128 devices in a mesh: gx: 4 (over y), gy: 32 (over x, z, core).
Axes of the slice: x: 4, y: 4, z: 4, core: 2. Of those that a mesh axis runs over, the one named last changes fastest.
Arguments:
- populations: float32 [512, 19, 32, 1024], P(('gx', 'gy')), may hold values from 0.5 to 1.5
- solid_share: float32 [512, 32, 1024], P(('gx', 'gy')), may hold values from 0 to 0.8
- migration: int32 [512], P(('gx', 'gy')), may hold values from 0 to 511, as said below
- neighbours: int32 [512, 8], P(('gx', 'gy')), may hold values from 0 to 511, as said below
Outputs:
- passed: float32 [512, 19, 32, 1024], P(('gx', 'gy'))
The draws below stay inside these ranges and needn't reach their ends.
Inputs may be any that keep to these rules, and one draw needn't show every extreme that they name: `migration`: A permutation of the slots; slot s lies on device s // 4 of the flattened gx+gy index. A block keeps its slot or moves into the freed slot of the device whose index differs in the lowest bit; each device hands over at most one block and receives exactly as many as it hands over. `neighbours`: the blocks form a strip of 4 columns and as many rows as devices, periodic both ways; the blocks of rows 2k and 2k+1 occupy the slots of devices 2k and 2k+1 in any order, before and after migration. So every listed neighbour slot, and the device that held that block before migration, lie on the row's own pair of devices or a pair beside it, within 3 devices along the flattened gx+gy index counted cyclically; the distance 3 occurs.
All inputs are finite; a program needn't handle non-finite values.
Results may differ from the reference program's by a relative error of at most 0.0003.
Values sent between devices are 32-bit elements; how exact they have to be, the bound alone decides.
No kernel may reach another device: no remote copies, remote signals or barrier semaphores. Data moves between devices by JAX's collectives and lax.ppermute only.
A program may use at most 192 MiB of HBM per device.

```python
import jax
import jax.numpy as jnp
import numpy as np
from jax import lax

BS = 32
Q = 19
BLK_DEV = 4
BLOCKS = 512


def force_place(place, order, pair, position, target):
    current = place[pair, position]
    other = order[pair, target]
    place = place.at[pair, other].set(current).at[pair, position].set(target)
    order = order.at[pair, current].set(other).at[pair, target].set(position)
    return (place, order)


def shared_plan(key):
    device_count = BLOCKS // BLK_DEV
    pair_count = device_count // 2
    span = 2 * BLK_DEV
    key_move, key_first, key_second, key_order = jax.random.split(jax.random.fold_in(key, 17), 4)
    moving = jax.random.randint(key_move, (pair_count,), 0, 2).astype(jnp.int32)
    moving = moving.at[0].set(1).at[1].set(1)
    first_pick = jax.random.randint(key_first, (pair_count,), 0, BLK_DEV).astype(jnp.int32)
    second_pick = jax.random.randint(key_second, (pair_count,), 0, BLK_DEV).astype(jnp.int32)
    slot_ids = jnp.arange(BLOCKS, dtype=jnp.int32)
    column = slot_ids // BLK_DEV
    across = slot_ids % BLK_DEV
    pair_index = column // 2
    odd_side = column % 2
    chosen = jnp.where(odd_side == 0, first_pick[pair_index], second_pick[pair_index])
    leaving = (moving[pair_index] == 1) & (across == chosen)
    partner = jnp.where(odd_side == 0, (column + 1) * BLK_DEV + second_pick[pair_index], (column - 1) * BLK_DEV + first_pick[pair_index])
    new_slot = jnp.where(leaving, partner, slot_ids).astype(jnp.int32)
    scores = jax.random.randint(key_order, (pair_count, span), 0, 1 << 20).astype(jnp.int32) * span + jnp.arange(span, dtype=jnp.int32)[None, :]
    order = jnp.argsort(scores, axis=1).astype(jnp.int32)
    place = jnp.argsort(order, axis=1).astype(jnp.int32)
    place, order = force_place(place, order, 0, BLK_DEV, 0)
    place, order = force_place(place, order, 1, 0, BLK_DEV)
    final_slot = (jnp.arange(pair_count, dtype=jnp.int32)[:, None] * span + place).reshape(BLOCKS).astype(jnp.int32)
    strip_row = slot_ids // BLK_DEV
    strip_col = slot_ids % BLK_DEV
    step_x = jnp.asarray([1, -1, 0, 0, 1, -1, 1, -1], jnp.int32)
    step_y = jnp.asarray([0, 0, 1, -1, 1, -1, -1, 1], jnp.int32)
    near_place = (strip_row[:, None] + step_y[None, :]) % device_count * BLK_DEV + (strip_col[:, None] + step_x[None, :]) % BLK_DEV
    table_after = jnp.zeros((BLOCKS, 8), jnp.int32).at[final_slot].set(final_slot[near_place])
    return (new_slot, table_after)


def draw_migration(key, part):
    new_slot, table_after = shared_plan(key)
    return new_slot


def draw_neighbours(key, part):
    new_slot, table_after = shared_plan(key)
    return table_after


def steps_of(stream_key, shape, shards, least, high):
    gain = 1.0
    for dim, shards_of in shards:
        steps = jax.random.uniform(jax.random.fold_in(jax.random.fold_in(stream_key, 6), dim), (shards_of,), jnp.float32, least / len(shards), high / len(shards))
        gain = gain * jnp.repeat(jnp.exp(steps), shape[dim] // shards_of).reshape((-1,) + (1,) * (len(shape) - 1 - dim))
    return gain


def setup_inputs(seed: int = 0) -> dict:
    arg_keys = jax.random.split(jax.random.key(seed), 5)
    return {
        "populations": jnp.clip(0.5 + 1.0 * jax.random.uniform(arg_keys[0], (BLOCKS, Q, BS, BS * BS), jnp.float32) ** steps_of(arg_keys[0], (BLOCKS, Q, BS, BS * BS), ((0, 128),), -0.2, 0.2), 0.5, 1.5),
        "solid_share": jnp.clip(0.8 * jax.random.uniform(arg_keys[1], (BLOCKS, BS, BS * BS), jnp.float32) ** steps_of(arg_keys[1], (BLOCKS, BS, BS * BS), ((0, 128),), -0.2, 0.2), 0.0, 0.8),
        "migration": draw_migration(jax.random.fold_in(arg_keys[4], 71), 0),
        "neighbours": draw_neighbours(jax.random.fold_in(arg_keys[4], 71), 0),
    }


VELOCITY = np.array([[0, 0, 0], [1, 0, 0], [-1, 0, 0], [0, 1, 0], [0, -1, 0], [0, 0, 1], [0, 0, -1],
                     [1, 1, 0], [-1, -1, 0], [1, -1, 0], [-1, 1, 0], [1, 0, 1], [-1, 0, -1], [1, 0, -1],
                     [-1, 0, 1], [0, 1, 1], [0, -1, -1], [0, 1, -1], [0, -1, 1]])
WEIGHT = np.array([1.0 / 3.0] + [1.0 / 18.0] * 6 + [1.0 / 36.0] * 12)
OPPOSITE = [0, 2, 1, 4, 3, 6, 5, 8, 7, 10, 9, 12, 11, 14, 13, 16, 15, 18, 17]


def relax_table():
    along_x = VELOCITY[:, 0] * 1.0
    along_y = VELOCITY[:, 1] * 1.0
    along_z = VELOCITY[:, 2] * 1.0
    energy = along_x * along_x + along_y * along_y + along_z * along_z
    normal_x = 2 * along_x * along_x - along_y * along_y - along_z * along_z
    normal_w = along_y * along_y - along_z * along_z
    rows = [np.ones(19), along_x, along_y, along_z, 19 * energy - 30, normal_x, normal_w,
            along_x * along_y, along_y * along_z, along_x * along_z,
            (5 * energy - 9) * along_x, (5 * energy - 9) * along_y, (5 * energy - 9) * along_z,
            along_x * (along_y * along_y - along_z * along_z),
            along_y * (along_z * along_z - along_x * along_x),
            along_z * (along_x * along_x - along_y * along_y),
            (21 * energy * energy - 53 * energy + 24) / 2,
            (3 * energy - 5) * normal_x, (3 * energy - 5) * normal_w]
    moments = np.stack(rows)
    rates = np.array([0, 0, 0, 0, 1.19, 1.6, 1.6, 1.6, 1.6, 1.6, 1.2, 1.2, 1.2, 1.98, 1.98, 1.98, 1.4, 1.4, 1.4])
    norms = np.sum(moments * moments, axis=1)
    return (moments.T * (rates / norms)[None, :]) @ moments


def collide(populations, solid_share):
    kind = populations.dtype
    velocity = jnp.asarray(VELOCITY * 1.0).astype(kind)
    weight = jnp.asarray(WEIGHT).astype(kind)
    relax_matrix = jnp.asarray(relax_table()).astype(kind)
    density = jnp.sum(populations, axis=1)
    speeds = []
    for column in range(3):
        flux = jnp.sum(populations * velocity[:, column][None, :, None, None], axis=1)
        speeds.append(flux / density)
    along = (velocity[:, 0][None, :, None, None] * speeds[0][:, None]
             + velocity[:, 1][None, :, None, None] * speeds[1][:, None]
             + velocity[:, 2][None, :, None, None] * speeds[2][:, None])
    square = speeds[0] * speeds[0] + speeds[1] * speeds[1] + speeds[2] * speeds[2]
    equilibrium = weight[None, :, None, None] * density[:, None] * (
        1.0 + 3.0 * along + 4.5 * along * along - 1.5 * square[:, None])
    relaxed = populations - jnp.einsum('ij,bjxv->bixv', relax_matrix, populations - equilibrium,
                                       precision=lax.Precision.HIGHEST)
    mirrored = populations[:, jnp.asarray(OPPOSITE, jnp.int32)]
    share = solid_share[:, None]
    return (1.0 - share) * relaxed + share * mirrored


def stream_pad(inner, face_got, edge_got, face_comps, edge_comps):
    count_blocks, comps, side = inner.shape[0], inner.shape[1], inner.shape[2]
    cube = inner.reshape(count_blocks, comps, side, side, side)
    padded = jnp.zeros((count_blocks, comps, side + 2, side + 2, side), inner.dtype)
    padded = padded.at[:, :, 1:side + 1, 1:side + 1, :].set(cube)
    fulls = []
    for index in range(4):
        whole = jnp.zeros((count_blocks, comps, side, side), inner.dtype)
        piece = face_got[:, index].reshape(count_blocks, len(face_comps[index]), side, side)
        fulls.append(whole.at[:, jnp.asarray(face_comps[index], jnp.int32)].set(piece))
    padded = padded.at[:, :, side + 1, 1:side + 1, :].set(fulls[0])
    padded = padded.at[:, :, 0, 1:side + 1, :].set(fulls[1])
    padded = padded.at[:, :, 1:side + 1, side + 1, :].set(fulls[2])
    padded = padded.at[:, :, 1:side + 1, 0, :].set(fulls[3])
    lines = []
    for index in range(4):
        whole = jnp.zeros((count_blocks, comps, side), inner.dtype)
        lines.append(whole.at[:, jnp.asarray(edge_comps[index], jnp.int32)].set(edge_got[:, index]))
    padded = padded.at[:, :, side + 1, side + 1, :].set(lines[0])
    padded = padded.at[:, :, 0, 0, :].set(lines[1])
    padded = padded.at[:, :, side + 1, 0, :].set(lines[2])
    padded = padded.at[:, :, 0, side + 1, :].set(lines[3])
    results = []
    for component in range(comps):
        step_x, step_y, step_z = int(VELOCITY[component, 0]), int(VELOCITY[component, 1]), int(VELOCITY[component, 2])
        window = padded[:, component, 1 - step_x:1 - step_x + side, 1 - step_y:1 - step_y + side, :]
        results.append(jnp.roll(window, step_z, axis=-1))
    return jnp.stack(results, axis=1).reshape(count_blocks, comps, side, side * side)


def reference(populations, solid_share, migration, neighbours):
    comps, side = populations.shape[1], populations.shape[2]
    moved = jnp.zeros_like(populations).at[migration].set(populations)
    moved_share = jnp.zeros_like(solid_share).at[migration].set(solid_share)

    def collide_one(item):
        return collide(item[0][None], item[1][None])[0]

    post = lax.map(collide_one, (moved, moved_share))
    every = list(range(comps))

    def stream_one(item):
        slot, near_slots = item

        def cube_of(index):
            return post[index].reshape(comps, side, side, side)

        face_got = jnp.stack([cube_of(near_slots[0])[:, 0].reshape(comps, side * side),
                              cube_of(near_slots[1])[:, side - 1].reshape(comps, side * side),
                              cube_of(near_slots[2])[:, :, 0].reshape(comps, side * side),
                              cube_of(near_slots[3])[:, :, side - 1].reshape(comps, side * side)])[None]
        edge_got = jnp.stack([cube_of(near_slots[4])[:, 0, 0], cube_of(near_slots[5])[:, side - 1, side - 1],
                              cube_of(near_slots[6])[:, 0, side - 1], cube_of(near_slots[7])[:, side - 1, 0]])[None]
        inner = post[slot][None]
        return stream_pad(inner, face_got, edge_got, [every] * 4, [every] * 4)[0]

    return lax.map(stream_one, (jnp.arange(BLOCKS, dtype=jnp.int32), neighbours))
```

```python
import jax
import jax.numpy as jnp
from jax import lax
from jax.experimental import pallas as pl
from jax.experimental.pallas import tpu as pltpu
from jax.sharding import PartitionSpec as P

VELOCITY = [
    (0, 0, 0), (1, 0, 0), (-1, 0, 0), (0, 1, 0), (0, -1, 0), (0, 0, 1), (0, 0, -1),
    (1, 1, 0), (-1, -1, 0), (1, -1, 0), (-1, 1, 0), (1, 0, 1), (-1, 0, -1), (1, 0, -1),
    (-1, 0, 1), (0, 1, 1), (0, -1, -1), (0, 1, -1), (0, -1, 1),
]
XP = [1, 7, 9, 11, 13]
XM = [2, 10, 8, 14, 12]
YU = [3, 7, 10, 15, 17]
YD = [4, 8, 9, 16, 18]
RANGES = [(3, 2), (7, 4), (15, 4)]
F32 = jnp.float32
ANY = pl.BlockSpec(memory_space=pl.ANY)
SMEM = pl.BlockSpec(memory_space=pltpu.SMEM)
FX_AT, FY_AT, TAG_AT, MATE_TILES = 76, 81, 86, 87


def collide(f, share):
    q = 1.0 - share
    s = [None] * 19
    d = [None] * 19
    for i in range(1, 19, 2):
        s[i] = f[i] + f[i + 1]
        d[i] = f[i] - f[i + 1]
    dxy, exy = s[7] + s[9], s[7] - s[9]
    dxz, exz = s[11] + s[13], s[11] - s[13]
    dyz, eyz = s[15] + s[17], s[15] - s[17]
    sx = (s[1] + s[3]) + s[5]
    sd = (dxy + dxz) + dyz
    rho = (f[0] + sx) + sd
    axy, bxy = d[7] + d[9], d[7] - d[9]
    axz, bxz = d[11] + d[13], d[11] - d[13]
    ayz, byz = d[15] + d[17], d[15] - d[17]
    tx, ty, tz = axy + axz, bxy + ayz, bxz + byz
    jx, jy, jz = d[1] + tx, d[3] + ty, d[5] + tz
    r = pl.reciprocal(rho, approx=True)
    r = r * (2.0 - rho * r)
    vx, vy, vz = jx * r, jy * r, jz * r
    ux, uy, uz = jx * vx, jy * vy, jz * vz
    j2 = (ux + uy) + uz
    iso_a = (-173.0 / 1800.0) * f[0] + (-4.0 / 45.0) * sx + ((-29.0 / 600.0) * sd + (197.0 / 1800.0) * j2)
    iso_d = (-23.0 / 900.0) * f[0] + (-1.0 / 36.0) * sx + ((-19.0 / 300.0) * sd + (-103.0 / 900.0) * j2)
    iso_0 = (53.0 / 60.0) * f[0] + (-7.0 / 15.0) * sx + ((-5.0 / 12.0) * sd + 0.65 * j2)

    def axis_even(x, dd, u):
        return q * ((11.0 / 15.0) * x + (-1.0 / 30.0) * dd + ((-23.0 / 60.0) * u + iso_a))

    def plane_even(x, dd, u):
        return q * ((-1.0 / 30.0) * x + (23.0 / 60.0) * dd + ((5.0 / 24.0) * u + iso_d))

    q4 = 0.4 * q
    q2 = 0.2 * q
    qm = 0.2475 * q
    ex, ey, ez = axis_even(s[1], dyz, ux), axis_even(s[3], dxz, uy), axis_even(s[5], dxy, uz)
    pyz, pxz, pxy = plane_even(s[1], dyz, ux), plane_even(s[3], dxz, uy), plane_even(s[5], dxy, uz)
    hxy, hxz, hyz = q4 * (exy - jx * vy), q4 * (exz - jx * vz), q4 * (eyz - jy * vz)
    hx = q2 * ((d[1] + d[1]) - tx)
    hy = q2 * ((d[3] + d[3]) - ty)
    hz = q2 * ((d[5] + d[5]) - tz)
    gx, gy, gz = 0.25 * hx, 0.25 * hy, 0.25 * hz
    mx, my, mz = qm * (axy - axz), qm * (ayz - bxy), qm * (bxz - byz)
    axy_o, bxy_o = mx - gx, -(my + gy)
    axz_o, bxz_o = -(mx + gx), mz - gz
    ayz_o, byz_o = my - gy, -(mz + gz)
    odd = {
        1: hx, 3: hy, 5: hz,
        7: axy_o + bxy_o, 9: axy_o - bxy_o,
        11: axz_o + bxz_o, 13: axz_o - bxz_o,
        15: ayz_o + byz_o, 17: ayz_o - byz_o,
    }
    even = {
        1: ex, 3: ey, 5: ez,
        7: pxy + hxy, 9: pxy - hxy,
        11: pxz + hxz, 13: pxz - hxz,
        15: pyz + hyz, 17: pyz - hyz,
    }
    post = [None] * 19
    post[0] = f[0] - q * iso_0
    for i in range(1, 19, 2):
        w = odd[i] + share * d[i]
        post[i] = (f[i] - even[i]) - w
        post[i + 1] = (f[i + 1] - even[i]) + w
    return post


def lane_masks():
    lane = lax.broadcasted_iota(jnp.int32, (8, 128), 1)
    depth = lane & 31
    return lane, depth == 0, depth == 31


def turn(x, step_y, step_z, first, last):
    if step_z == 0:
        return x if step_y == 0 else pltpu.roll(x, (32 * step_y) % 128, 1)
    flat = 32 * step_y + step_z
    wrap = flat - 32 * step_z
    edge = first if step_z == 1 else last
    return jnp.where(edge, pltpu.roll(x, wrap % 128, 1), pltpu.roll(x, flat % 128, 1))


def unit(source, result, column, masks):
    lane, first, last = masks
    for part in range(4):
        rows = pl.ds(8 * part, 8)
        post = collide([source[c, rows, :] for c in range(19)], source[19, rows, :])
        for c in range(19):
            step_x, step_y, step_z = VELOCITY[c]
            value = turn(post[c], step_y, step_z, first, last)
            to = pl.ds(8 + 8 * part + step_x, 8)
            if step_y == 0:
                result[c, column + 1, to, :] = value
            else:
                out = (lane < 32) if step_y == 1 else (lane >= 96)
                pltpu.store(result.at[c, column + 1, to, :], value, mask=jnp.logical_not(out))
                pltpu.store(result.at[c, column + 1 + step_y, to, :], value, mask=out)


def device_index():
    return lax.axis_index("gx") * lax.axis_size("gy") + lax.axis_index("gy")


def leaver_of(migration):
    base = device_index() * 4
    leaver = jnp.int32(0)
    moving = jnp.bool_(False)
    for b in (3, 2, 1, 0):
        away = migration[b] != base + b
        leaver = jnp.where(away, b, leaver)
        moving = jnp.logical_or(moving, away)
    return leaver, moving


def column_copy(pop, share, block, column, dest, sem_p, sem_s):
    lanes = pl.ds(pl.multiple_of(column * 128, 128), 128)
    return (
        pltpu.make_async_copy(pop.at[block, :, :, lanes], dest.at[pl.ds(0, 19)], sem_p),
        pltpu.make_async_copy(share.at[block, :, lanes], dest.at[19], sem_s),
    )


def first_kernel(migration, pop, share, mate, rise, fall,
                 units, streamed, sides, rows, face, rise_v, fall_v,
                 unit_p, unit_s, side_p, side_s, row_p, row_s, out_sem, face_sem):
    masks = lane_masks()
    lane, first, last = masks
    leaver, _ = leaver_of(migration)

    def side_copies(b, high):
        return column_copy(pop, share, b, 7 * high, sides.at[high, b], side_p.at[high, b], side_s.at[high, b])

    def row_copies(b, low):
        at = pl.ds(0 if low else 31, 1)
        to = pl.ds(4 * low + b, 1)
        return (
            pltpu.make_async_copy(pop.at[b, :, at, :], rows.at[pl.ds(0, 19), to, :], row_p.at[low, b]),
            pltpu.make_async_copy(share.at[b, at, :], rows.at[19, to, :], row_s.at[low, b]),
        )

    def unit_copies(v):
        return column_copy(pop, share, leaver, v, units.at[v], unit_p.at[v], unit_s.at[v])

    for b in range(4):
        for side in range(2):
            for cp in side_copies(b, side):
                cp.start()
    for b in range(4):
        for side in range(2):
            for cp in row_copies(b, side):
                cp.start()

    def begin(v, carry):
        for cp in unit_copies(v):
            cp.start()
        return carry

    lax.fori_loop(0, 8, begin, 0)

    segment = lane // 32
    tag = jnp.zeros((8, 128), F32)
    for b in range(4):
        tag = jnp.where(segment == b, jnp.full((8, 128), migration[b], jnp.int32).astype(F32), tag)
    for v in range(8):
        face[10, :, pl.ds(128 * v, 128)] = tag
    for v in range(4):
        rise_v[5, :, pl.ds(128 * v, 128)] = tag
        fall_v[5, :, pl.ds(128 * v, 128)] = tag

    for high in (0, 1):
        for b in range(4):
            for cp in side_copies(b, high):
                cp.wait()
        comps = YU if high else YD
        for part in range(4):
            at = pl.ds(8 * part, 8)

            def packed(c):
                got = None
                for b in range(4):
                    shift = (32 * (b - 3)) % 128 if high else 32 * b
                    x = sides[high, b, c, at, :]
                    x = pltpu.roll(x, shift, 1) if shift else x
                    got = x if got is None else jnp.where(segment == b, x, got)
                return got

            post = collide([packed(c) for c in range(19)], packed(19))
            for i, c in enumerate(comps):
                value = turn(post[c], 0, VELOCITY[c][2], first, last)
                face[5 + i, :, pl.ds(128 * (part + 4 * (1 - high)), 128)] = value
                (rise_v if high else fall_v)[i, :, pl.ds(128 * part, 128)] = value

    for b in range(4):
        for side in range(2):
            for cp in row_copies(b, side):
                cp.wait()
    upper = lax.broadcasted_iota(jnp.int32, (8, 128), 0) < 4
    for v in range(8):
        at = pl.ds(128 * v, 128)
        post = collide([rows[c, :, at] for c in range(19)], rows[19, :, at])
        for i in range(5):
            value = jnp.where(upper, post[XP[i]], post[XM[i]])
            _, step_y, step_z = VELOCITY[XP[i]]
            value = turn(value, step_y, step_z, first, last)
            if step_y == 0:
                face[i, :, at] = value
            else:
                out = (lane < 32) if step_y == 1 else (lane >= 96)
                pltpu.store(face.at[i, :, at], value, mask=jnp.logical_not(out))
                beside = (v + step_y) % 8
                pltpu.store(face.at[i, :, pl.ds(128 * beside, 128)], value, mask=out)

    ends = [
        pltpu.make_async_copy(face, mate.at[pl.ds(FX_AT, 11)], face_sem.at[0]),
        pltpu.make_async_copy(rise_v, rise, face_sem.at[1]),
        pltpu.make_async_copy(fall_v, fall, face_sem.at[2]),
    ]
    for cp in ends:
        cp.start()

    def send(v):
        lanes = pl.ds(pl.multiple_of(v * 128, 128), 128)
        return [
            pltpu.make_async_copy(
                streamed.at[:, v + 1, pl.ds(8 + 8 * part, 8), :],
                mate.at[pl.ds(19 * part, 19), :, lanes],
                out_sem.at[v, part],
            )
            for part in range(4)
        ]

    def body(v, carry):
        for cp in unit_copies(v):
            cp.wait()
        unit(units.at[v], streamed, v, masks)

        @pl.when(v > 0)
        def _():
            for cp in send(v - 1):
                cp.start()

        return carry

    lax.fori_loop(0, 8, body, 0)
    for cp in send(7):
        cp.start()

    def finish(v, carry):
        for cp in send(v):
            cp.wait()
        return carry

    lax.fori_loop(0, 8, finish, 0)
    for cp in ends:
        cp.wait()


def second_kernel(migration, pop, share, after, out, units, streamed, unit_p, unit_s, out_sem):
    masks = lane_masks()
    leaver, _ = leaver_of(migration)

    def block(j):
        return j + (j >= leaver).astype(jnp.int32)

    def copies(u):
        return column_copy(pop, share, block(u // 8), u % 8, units.at[u], unit_p.at[u], unit_s.at[u])

    def send(u):
        lanes = pl.ds(pl.multiple_of((u % 8) * 128, 128), 128)
        return pltpu.make_async_copy(
            streamed.at[u // 8, :, u % 8 + 1, pl.ds(8, 32), :],
            out.at[block(u // 8), :, :, lanes],
            out_sem.at[u],
        )

    def begin(u, carry):
        for cp in copies(u):
            cp.start()
        return carry

    lax.fori_loop(0, 24, begin, 0)

    def body(u, carry):
        for cp in copies(u):
            cp.wait()
        unit(units.at[u], streamed.at[u // 8], u % 8, masks)

        @pl.when(u % 8 > 0)
        def _():
            send(u - 1).start()

        @pl.when(u % 8 == 7)
        def _():
            send(u).start()

        return carry

    lax.fori_loop(0, 24, body, 0)

    def finish(u, carry):
        send(u).wait()
        return carry

    lax.fori_loop(0, 24, finish, 0)


def third_kernel(neighbours, migration, mine, got, low_a, low_b, high_a, high_b, out_in, out,
                 filled, sides, fx, fy, tags, table,
                 fill_sem, side_sem, face_sem, tag_sem, row_sem):
    del out_in
    base = device_index() * 4
    pair = base // 8 * 8
    leaver, moving = leaver_of(migration)
    lane = lax.broadcasted_iota(jnp.int32, (8, 128), 1)
    sub = lax.broadcasted_iota(jnp.int32, (8, 128), 0)

    def block(j):
        return j + (j >= leaver).astype(jnp.int32)

    def fills(source):
        return [
            pltpu.make_async_copy(source.at[pl.ds(19 * part, 19)], filled.at[part], fill_sem.at[part])
            for part in range(4)
        ]

    tag_copies = [pltpu.make_async_copy(got.at[TAG_AT, pl.ds(0, 1), pl.ds(0, 128)], tags.at[pl.ds(0, 1)], tag_sem.at[0])]
    for k, ref in enumerate((low_a, low_b, high_a, high_b)):
        tag_copies.append(
            pltpu.make_async_copy(ref.at[5, pl.ds(0, 1), pl.ds(0, 128)], tags.at[pl.ds(k + 1, 1)], tag_sem.at[k + 1])
        )
    face_copies = [
        pltpu.make_async_copy(mine.at[pl.ds(FX_AT, 5)], fx.at[0], face_sem.at[0]),
        pltpu.make_async_copy(got.at[pl.ds(FX_AT, 5)], fx.at[1], face_sem.at[1]),
        pltpu.make_async_copy(mine.at[pl.ds(FY_AT, 5)], fy.at[0], face_sem.at[2]),
        pltpu.make_async_copy(got.at[pl.ds(FY_AT, 5)], fy.at[1], face_sem.at[3]),
    ]
    for k, ref in enumerate((low_a, low_b, high_a, high_b)):
        lanes = pl.ds(0 if k < 2 else 512, 512)
        face_copies.append(
            pltpu.make_async_copy(ref.at[pl.ds(0, 5)], fy.at[k + 2, :, :, lanes], face_sem.at[k + 4])
        )
    for cp in tag_copies + face_copies:
        cp.start()

    @pl.when(moving)
    def _():
        for cp in fills(got):
            cp.start()

    @pl.when(jnp.logical_not(moving))
    def _():
        for cp in fills(mine):
            cp.start()

    def side_copies(j, back):
        made = []
        for high in range(2):
            at = 0
            for k, (start, size) in enumerate(RANGES):
                there = out.at[block(j), pl.ds(start, size), :, pl.ds(896 * high, 128)]
                here = sides.at[j, high, pl.ds(at, size)]
                sem = side_sem.at[j, high, k]
                made.append(pltpu.make_async_copy(here, there, sem) if back else pltpu.make_async_copy(there, here, sem))
                at += size
        return made

    for j in range(3):
        for cp in side_copies(j, False):
            cp.start()

    for cp in tag_copies:
        cp.wait()
    for b in range(4):
        table[migration[b] & 7] = b
        table[tags[0, 32 * b].astype(jnp.int32) & 7] = 4 + b
        for k in range(4):
            table[(8 if k < 2 else 16) + (tags[k + 1, 32 * b].astype(jnp.int32) & 7)] = 4 * (k + 2) + b

    def find(b, k, beside):
        slot = neighbours[b, k]
        code = table[(slot & 7) + jnp.where(slot // 8 * 8 == pair, 0, beside)]
        return code // 4, code % 4

    for cp in face_copies:
        cp.wait()

    def with_row(now, where, step_x, k, column):
        src, j = where
        home, start = (0, 0) if step_x == 1 else (7, 4)
        row = pltpu.roll(fx[src, k, :, pl.ds(128 * column, 128)], (home + 8 - start - j) % 8, 0)
        return jnp.where(sub == home, row, now)

    def patch(b, read, write):
        xs = {1: find(b, 1, 0), -1: find(b, 0, 0)}
        corners = {
            (1, 1): find(b, 5, 8), (-1, 1): find(b, 6, 8),
            (-1, -1): find(b, 4, 16), (1, -1): find(b, 7, 16),
        }
        for high in (0, 1):
            flow = -1 if high else 1
            comps = YD if high else YU
            home = 3 if high else 0
            source, at = find(b, 2 if high else 3, 16 if high else 8)

            def tile(where, i, part):
                src, j = where
                x = fy[src, i, :, pl.ds(128 * (part + 4 * high), 128)]
                return pltpu.roll(x, (32 * (home + 4 - j)) % 128, 1)

            edge = (lane >= 96) if high else (lane < 32)
            for c in (3, 4, 7, 8, 9, 10, 15, 16, 17, 18):
                step_x, step_y, _ = VELOCITY[c]
                in_y = step_y == flow
                if not in_y and step_x == 0:
                    continue
                if in_y:
                    i = comps.index(c)
                    tiles = [tile((source, at), i, part) for part in range(4)]
                    if step_x == 1:
                        near = [tile(corners[(1, step_y)], i, 3)] + tiles
                        near = [pltpu.roll(t, 1, 0) for t in near]
                        tiles = [jnp.where(sub == 0, near[p], near[p + 1]) for p in range(4)]
                    elif step_x == -1:
                        near = tiles + [tile(corners[(-1, step_y)], i, 0)]
                        near = [pltpu.roll(t, 7, 0) for t in near]
                        tiles = [jnp.where(sub == 7, near[p + 1], near[p]) for p in range(4)]
                for part in range(4):
                    in_x = (step_x == 1 and part == 0) or (step_x == -1 and part == 3)
                    if not in_y and not in_x:
                        continue
                    now = read(c, part, high)
                    if in_x:
                        k = (XP if step_x == 1 else XM).index(c)
                        now = with_row(now, xs[step_x], step_x, k, 7 * high)
                    if in_y:
                        now = jnp.where(edge, tiles[part], now)
                    write(c, part, high, now)
        return xs

    order = (3, 4, 7, 8, 9, 10, 15, 16, 17, 18)

    def row_copies(j, xs):
        made = []
        for step_x, comps in ((1, XP), (-1, XM)):
            src, at = xs[step_x]
            for k, c in enumerate(comps):
                lanes = pl.ds(0, 1024) if VELOCITY[c][1] == 0 else pl.ds(128, 768)
                made.append(
                    pltpu.make_async_copy(
                        fx.at[src, k, pl.ds(at + (0 if step_x == 1 else 4), 1), lanes],
                        out.at[block(j), c, pl.ds(0 if step_x == 1 else 31, 1), lanes],
                        row_sem.at[j, k + (0 if step_x == 1 else 5)],
                    )
                )
        return made

    pending = []
    for j in range(3):
        b = block(j)
        for cp in side_copies(j, False):
            cp.wait()

        def read(c, part, high, j=j):
            return sides[j, high, order.index(c), pl.ds(8 * part, 8), :]

        def write(c, part, high, value, j=j):
            sides[j, high, order.index(c), pl.ds(8 * part, 8), :] = value

        xs = patch(b, read, write)
        made = row_copies(j, xs) + side_copies(j, True)
        for cp in made:
            cp.start()
        pending += made

    for cp in fills(got):
        cp.wait()

    def read_filled(c, part, high):
        return filled[part, c, :, pl.ds(896 * high, 128)]

    def write_filled(c, part, high, value):
        filled[part, c, :, pl.ds(896 * high, 128)] = value

    xs = patch(leaver, read_filled, write_filled)
    for step_x, comps in ((1, XP), (-1, XM)):
        part = 0 if step_x == 1 else 3
        for k, c in enumerate(comps):
            for column in range(8) if VELOCITY[c][1] == 0 else range(1, 7):
                lanes = pl.ds(128 * column, 128)
                filled[part, c, :, lanes] = with_row(filled[part, c, :, lanes], xs[step_x], step_x, k, column)
    for part in range(4):
        cp = pltpu.make_async_copy(filled.at[part], out.at[leaver, :, pl.ds(8 * part, 8), :], fill_sem.at[part])
        cp.start()
        pending.append(cp)
    for cp in pending:
        cp.wait()


def route(shift, cross):
    count = lax.axis_size("gx") * lax.axis_size("gy")
    return [(d, ((d + shift) % count) ^ cross) for d in range(count)]


def on_device(populations, solid_share, migration, neighbours):
    limit = 56 * 2**20
    dma = pltpu.SemaphoreType.DMA
    mate, rise, fall = pl.pallas_call(
        first_kernel,
        name="faces_and_leaver",
        out_shape=(
            jax.ShapeDtypeStruct((MATE_TILES, 8, 1024), F32),
            jax.ShapeDtypeStruct((6, 8, 512), F32),
            jax.ShapeDtypeStruct((6, 8, 512), F32),
        ),
        in_specs=[SMEM, ANY, ANY],
        out_specs=(ANY, ANY, ANY),
        scratch_shapes=[
            pltpu.VMEM((8, 20, 32, 128), F32),
            pltpu.VMEM((19, 10, 48, 128), F32),
            pltpu.VMEM((2, 4, 20, 32, 128), F32),
            pltpu.VMEM((20, 8, 1024), F32),
            pltpu.VMEM((11, 8, 1024), F32),
            pltpu.VMEM((6, 8, 512), F32),
            pltpu.VMEM((6, 8, 512), F32),
            dma((8,)), dma((8,)), dma((2, 4)), dma((2, 4)), dma((2, 4)), dma((2, 4)), dma((8, 4)), dma((3,)),
        ],
        compiler_params=pltpu.CompilerParams(vmem_limit_bytes=limit),
        cost_estimate=pl.CostEstimate(flops=20_000_000, bytes_accessed=9_000_000, transcendentals=0),
    )(migration, populations, solid_share)

    axes = ("gx", "gy")
    got = lax.ppermute(mate, axes, route(0, 1))
    low_a = lax.ppermute(rise, axes, route(2, 0))
    high_a = lax.ppermute(fall, axes, route(-2, 0))
    low_b = lax.ppermute(rise, axes, route(2, 1))
    high_b = lax.ppermute(fall, axes, route(-2, 1))

    out = pl.pallas_call(
        second_kernel,
        name="staying_blocks",
        out_shape=jax.ShapeDtypeStruct((4, 19, 32, 1024), F32),
        in_specs=[SMEM, ANY, ANY, ANY],
        out_specs=ANY,
        scratch_shapes=[
            pltpu.VMEM((24, 20, 32, 128), F32),
            pltpu.VMEM((3, 19, 10, 48, 128), F32),
            dma((24,)), dma((24,)), dma((24,)),
        ],
        compiler_params=pltpu.CompilerParams(vmem_limit_bytes=limit),
        cost_estimate=pl.CostEstimate(flops=30_000_000, bytes_accessed=16_000_000, transcendentals=0),
    )(migration, populations, solid_share, rise)

    return pl.pallas_call(
        third_kernel,
        name="patch_boundaries",
        out_shape=jax.ShapeDtypeStruct((4, 19, 32, 1024), F32),
        in_specs=[SMEM, SMEM] + [ANY] * 7,
        out_specs=ANY,
        input_output_aliases={8: 0},
        scratch_shapes=[
            pltpu.VMEM((4, 19, 8, 1024), F32),
            pltpu.VMEM((3, 2, 10, 32, 128), F32),
            pltpu.VMEM((2, 5, 8, 1024), F32),
            pltpu.VMEM((6, 5, 8, 1024), F32),
            pltpu.SMEM((5, 128), F32),
            pltpu.SMEM((24,), jnp.int32),
            dma((4,)), dma((3, 2, 3)), dma((8,)), dma((5,)), dma((3, 10)),
        ],
        compiler_params=pltpu.CompilerParams(vmem_limit_bytes=limit),
        cost_estimate=pl.CostEstimate(flops=1_000_000, bytes_accessed=8_000_000, transcendentals=0),
    )(neighbours, migration, mate, got, low_a, low_b, high_a, high_b, out)


def solution(mesh):
    return jax.shard_map(
        on_device,
        mesh=mesh,
        in_specs=(
            P(("gx", "gy"), None, None, None),
            P(("gx", "gy"), None, None),
            P(("gx", "gy")),
            P(("gx", "gy"), None),
        ),
        out_specs=P(("gx", "gy"), None, None, None),
        check_vma=False,
    )
```

```python
import jax
import jax.numpy as jnp
from jax import lax
from jax.experimental import pallas as pl
from jax.experimental.pallas import tpu as pltpu
from jax.sharding import PartitionSpec as P

VELOCITY = [
    (0, 0, 0), (1, 0, 0), (-1, 0, 0), (0, 1, 0), (0, -1, 0), (0, 0, 1), (0, 0, -1),
    (1, 1, 0), (-1, -1, 0), (1, -1, 0), (-1, 1, 0), (1, 0, 1), (-1, 0, -1), (1, 0, -1),
    (-1, 0, 1), (0, 1, 1), (0, -1, -1), (0, 1, -1), (0, -1, 1),
]
XP = [1, 7, 9, 11, 13]
XM = [2, 10, 8, 14, 12]
YU = [3, 7, 10, 15, 17]
YD = [4, 8, 9, 16, 18]
F32 = jnp.float32
LIMITS = (12, 8, 12)
HBM = pl.BlockSpec(memory_space=pltpu.HBM)
VMEM = pl.BlockSpec(memory_space=pltpu.VMEM)
SMEM = pl.BlockSpec(memory_space=pltpu.SMEM)
FX_AT, FU_AT, FD_AT, TAG_AT, MATE = 152, 162, 167, 172, 173


def collide(f, share):
    q = 1.0 - share
    s = [None] * 19
    d = [None] * 19
    for i in range(1, 19, 2):
        s[i] = f[i] + f[i + 1]
        d[i] = f[i] - f[i + 1]
    dxy, exy = s[7] + s[9], s[7] - s[9]
    dxz, exz = s[11] + s[13], s[11] - s[13]
    dyz, eyz = s[15] + s[17], s[15] - s[17]
    sx = (s[1] + s[3]) + s[5]
    sd = (dxy + dxz) + dyz
    rho = (f[0] + sx) + sd
    axy, bxy = d[7] + d[9], d[7] - d[9]
    axz, bxz = d[11] + d[13], d[11] - d[13]
    ayz, byz = d[15] + d[17], d[15] - d[17]
    tx, ty, tz = axy + axz, bxy + ayz, bxz + byz
    jx, jy, jz = d[1] + tx, d[3] + ty, d[5] + tz
    r = pl.reciprocal(rho, approx=True)
    r = r * (2.0 - rho * r)
    vx, vy, vz = jx * r, jy * r, jz * r
    ux, uy, uz = jx * vx, jy * vy, jz * vz
    j2 = (ux + uy) + uz
    iso_a = (-173.0 / 1800.0) * f[0] + (-4.0 / 45.0) * sx + ((-29.0 / 600.0) * sd + (197.0 / 1800.0) * j2)
    iso_d = (-23.0 / 900.0) * f[0] + (-1.0 / 36.0) * sx + ((-19.0 / 300.0) * sd + (-103.0 / 900.0) * j2)
    iso_0 = (53.0 / 60.0) * f[0] + (-7.0 / 15.0) * sx + ((-5.0 / 12.0) * sd + 0.65 * j2)

    def axis_even(x, dd, u):
        return q * ((11.0 / 15.0) * x + (-1.0 / 30.0) * dd + ((-23.0 / 60.0) * u + iso_a))

    def plane_even(x, dd, u):
        return q * ((-1.0 / 30.0) * x + (23.0 / 60.0) * dd + ((5.0 / 24.0) * u + iso_d))

    q4 = 0.4 * q
    q2 = 0.2 * q
    qm = 0.2475 * q
    ex, ey, ez = axis_even(s[1], dyz, ux), axis_even(s[3], dxz, uy), axis_even(s[5], dxy, uz)
    pyz, pxz, pxy = plane_even(s[1], dyz, ux), plane_even(s[3], dxz, uy), plane_even(s[5], dxy, uz)
    hxy, hxz, hyz = q4 * (exy - jx * vy), q4 * (exz - jx * vz), q4 * (eyz - jy * vz)
    hx = q2 * ((d[1] + d[1]) - tx)
    hy = q2 * ((d[3] + d[3]) - ty)
    hz = q2 * ((d[5] + d[5]) - tz)
    gx, gy, gz = 0.25 * hx, 0.25 * hy, 0.25 * hz
    mx, my, mz = qm * (axy - axz), qm * (ayz - bxy), qm * (bxz - byz)
    axy_o, bxy_o = mx - gx, -(my + gy)
    axz_o, bxz_o = -(mx + gx), mz - gz
    ayz_o, byz_o = my - gy, -(mz + gz)
    odd = {
        1: hx, 3: hy, 5: hz,
        7: axy_o + bxy_o, 9: axy_o - bxy_o,
        11: axz_o + bxz_o, 13: axz_o - bxz_o,
        15: ayz_o + byz_o, 17: ayz_o - byz_o,
    }
    even = {
        1: ex, 3: ey, 5: ez,
        7: pxy + hxy, 9: pxy - hxy,
        11: pxz + hxz, 13: pxz - hxz,
        15: pyz + hyz, 17: pyz - hyz,
    }
    post = [None] * 19
    post[0] = f[0] - q * iso_0
    for i in range(1, 19, 2):
        w = odd[i] + share * d[i]
        post[i] = (f[i] - even[i]) - w
        post[i + 1] = (f[i + 1] - even[i]) + w
    return post


def lane_tables():
    lane = lax.broadcasted_iota(jnp.int32, (8, 128), 1)
    tables = {}
    for step_y in (-1, 0, 1):
        for step_z in (-1, 1):
            tables[step_y, step_z] = ((lane - 32 * step_y) & 96) | ((lane - step_z) & 31)
    return lane, tables


def turn(x, step_y, step_z, tables):
    if step_z:
        return jnp.take_along_axis(x, tables[step_y, step_z], axis=1)
    return pltpu.roll(x, (32 * step_y) % 128, 1) if step_y else x


def unit(source, result, column, lanes_of):
    lane, tables = lanes_of
    at = pl.ds(pl.multiple_of(column * 128, 128), 128)
    for part in range(4):
        rows = pl.ds(8 * part, 8)
        post = collide([source[c, rows, at] for c in range(19)], source[19, rows, at])
        for c in range(19):
            step_x, step_y, step_z = VELOCITY[c]
            value = turn(post[c], step_y, step_z, tables)
            to = pl.ds(8 + 8 * part + step_x, 8)
            if step_y == 0:
                result[c, column + 1, to, :] = value
            else:
                out = (lane < 32) if step_y == 1 else (lane >= 96)
                pltpu.store(result.at[c, column + 1, to, :], value, mask=jnp.logical_not(out))
                pltpu.store(result.at[c, column + 1 + step_y, to, :], value, mask=out)


def device_index():
    return lax.axis_index("gx") * lax.axis_size("gy") + lax.axis_index("gy")


def leaver_of(migration):
    base = device_index() * 4
    leaver = jnp.int32(0)
    moving = jnp.bool_(False)
    for b in (3, 2, 1, 0):
        away = migration[b] != base + b
        leaver = jnp.where(away, b, leaver)
        moving = jnp.logical_or(moving, away)
    return leaver, moving


def staying(j, leaver):
    return j + (j >= leaver).astype(jnp.int32)


def early_blocks():
    return jnp.int32(1)


def first_kernel(migration, pop, share, raw, streamed, mate, rise, fall, leaving, pop_sem, share_sem, mate_sem):
    lanes_of = lane_tables()
    lane, tables = lanes_of
    leaver, _ = leaver_of(migration)

    def block(p):
        return jnp.where(p == 0, leaver, staying(p - 1, leaver))

    def load(p):
        return (
            pltpu.make_async_copy(pop.at[block(p)], raw.at[p, pl.ds(0, 19)], pop_sem.at[p]),
            pltpu.make_async_copy(share.at[block(p)], raw.at[p, 19], share_sem.at[p]),
        )

    for p in range(4):
        for cp in load(p):
            cp.start()

    segment = lane >> 5
    tag = jnp.zeros((8, 128), F32)
    for p in range(4):
        tag = jnp.where(segment == p, jnp.full((8, 128), migration[block(p)], jnp.int32).astype(F32), tag)
    mate[TAG_AT, pl.ds(0, 8), :] = tag
    rise[5, pl.ds(0, 8), :] = tag
    fall[5, pl.ds(0, 8), :] = tag

    def hand(v):
        return pltpu.make_async_copy(
            leaving.at[:, v + 1, pl.ds(8, 32), :], mate.at[pl.ds(19 * v, 19)], mate_sem.at[v]
        )

    for cp in load(0):
        cp.wait()

    def leaving_unit(v, carry):
        unit(raw.at[0], leaving, v, lanes_of)

        @pl.when(v > 0)
        def _():
            hand(v - 1).start()

        return carry

    lax.fori_loop(0, 8, leaving_unit, 0)
    hand(7).start()

    def early(j, carry):
        for cp in load(j + 1):
            cp.wait()

        def one(v, inner):
            unit(raw.at[j + 1], streamed.at[j], v, lanes_of)
            return inner

        return lax.fori_loop(0, 8, one, carry)

    lax.fori_loop(0, early_blocks(), early, 0)

    def rest(j, carry):
        for cp in load(j + 1):
            cp.wait()
        return carry

    lax.fori_loop(early_blocks(), 3, rest, 0)

    for high in (0, 1):
        column = pl.ds(896 * high, 128)
        for part in range(4):
            rows = pl.ds(8 * part, 8)

            def packed(c):
                got = None
                for p in range(4):
                    shift = (32 * (p - 3)) % 128 if high else 32 * p
                    x = raw[p, c, rows, column]
                    x = pltpu.roll(x, shift, 1) if shift else x
                    got = x if got is None else jnp.where(segment == p, x, got)
                return got

            post = collide([packed(c) for c in range(19)], packed(19))
            for i, c in enumerate(YU if high else YD):
                value = turn(post[c], 0, VELOCITY[c][2], tables)
                mate[(FU_AT if high else FD_AT) + i, rows, :] = value
                (rise if high else fall)[i, rows, :] = value

    sub = lax.broadcasted_iota(jnp.int32, (8, 128), 0)

    def x_faces(v, carry):
        column = pl.ds(pl.multiple_of(v * 128, 128), 128)

        def packed(c):
            got = None
            for p in range(4):
                x = pltpu.roll(raw[p, c, pl.ds(24, 8), column], (p + 1) % 8, 0)
                y = pltpu.roll(raw[p, c, pl.ds(0, 8), column], p + 4, 0)
                got = x if got is None else jnp.where(sub == p, x, got)
                got = jnp.where(sub == p + 4, y, got)
            return got

        post = collide([packed(c) for c in range(19)], packed(19))
        for i in range(5):
            value = jnp.where(sub < 4, post[XP[i]], post[XM[i]])
            _, step_y, step_z = VELOCITY[XP[i]]
            value = turn(value, step_y, step_z, tables)

            def place(v, k):
                return mate.at[FX_AT + 2 * i + (v >> 2), pl.ds(pl.multiple_of((v & 3) * 8, 8), 8), :]

            if step_y == 0:
                place(v, i)[...] = value
            else:
                out = (lane < 32) if step_y == 1 else (lane >= 96)
                pltpu.store(place(v, i), value, mask=jnp.logical_not(out))
                pltpu.store(place((v + step_y) & 7, i), value, mask=out)
        return carry

    lax.fori_loop(0, 8, x_faces, 0)
    for v in range(8):
        hand(v).wait()


def second_kernel(migration, raw, held, after, out, streamed, out_sem):
    del held, after
    lanes_of = lane_tables()
    leaver, _ = leaver_of(migration)

    def send(j, v):
        return pltpu.make_async_copy(
            streamed.at[j, :, v + 1, pl.ds(8, 32), :],
            out.at[staying(j, leaver), :, :, pl.ds(pl.multiple_of(v * 128, 128), 128)],
            out_sem.at[j, v],
        )

    def ready(j, carry):
        for v in range(1, 7):
            send(j, v).start()
        return carry

    lax.fori_loop(0, early_blocks(), ready, 0)

    def late(j, carry):
        def one(v, inner):
            unit(raw.at[j + 1], streamed.at[j], v, lanes_of)

            @pl.when(v > 1)
            def _():
                send(j, v - 1).start()

            return inner

        return lax.fori_loop(0, 8, one, carry)

    lax.fori_loop(early_blocks(), 3, late, 0)
    for j in range(3):
        for v in range(1, 7):
            send(j, v).wait()


def third_kernel(neighbours, migration, mine, low_a, low_b, high_a, high_b, got_in, held, out_in,
                 out, got, streamed, fx, fu, fd, rows, tags, table, tag_sem, got_sem, side_sem, row_sem):
    del got_in, held, out_in
    pair = (device_index() >> 1) << 3
    leaver, moving = leaver_of(migration)
    lane = lax.broadcasted_iota(jnp.int32, (8, 128), 1)
    sub = lax.broadcasted_iota(jnp.int32, (8, 128), 0)

    tag_copies = [pltpu.make_async_copy(got.at[TAG_AT, pl.ds(0, 1)], tags.at[pl.ds(0, 1)], tag_sem.at[0])]
    for k, ref in enumerate((low_a, low_b, high_a, high_b)):
        tag_copies.append(pltpu.make_async_copy(ref.at[5, pl.ds(0, 1)], tags.at[pl.ds(k + 1, 1)], tag_sem.at[k + 1]))
    for cp in tag_copies:
        cp.start()

    for s, ref in enumerate((mine, got)):
        fx[s] = ref[pl.ds(FX_AT, 10)]
        fu[s] = ref[pl.ds(FU_AT, 5)]
        fd[s] = ref[pl.ds(FD_AT, 5)]
    for s in range(2):
        fu[2 + s] = (low_a, low_b)[s][pl.ds(0, 5)]
        fd[2 + s] = (high_a, high_b)[s][pl.ds(0, 5)]

    @pl.when(jnp.logical_not(moving))
    def _():
        def keep(n, carry):
            got[n] = mine[n]
            return carry

        lax.fori_loop(0, FX_AT, keep, 0)

    for cp in tag_copies:
        cp.wait()
    for p in range(4):
        table[migration[leaver if p == 0 else staying(p - 1, leaver)] & 7] = p
        for k, (start, source) in enumerate(((0, 1), (8, 2), (8, 3), (16, 2), (16, 3))):
            table[start + (tags[k, 32 * p].astype(jnp.int32) & 7)] = 4 * source + p

    def find(b, k, beside):
        slot = neighbours[b, k]
        code = table[(slot & 7) + jnp.where((slot >> 3) << 3 == pair, 0, beside)]
        return code >> 2, code & 3

    def with_row(now, where, step_x, k, column):
        src, p = where
        home, start = (0, 0) if step_x == 1 else (7, 4)
        x = fx[src, 2 * k + column // 4, pl.ds(8 * (column % 4), 8), :]
        return jnp.where(sub == home, pltpu.roll(x, (home + 8 - start - p) & 7, 0), now)

    def patch_columns(b, xs, at):
        corners = {
            (1, 1): find(b, 5, 8), (-1, 1): find(b, 6, 8),
            (-1, -1): find(b, 4, 16), (1, -1): find(b, 7, 16),
        }
        for high in (0, 1):
            flow = -1 if high else 1
            comps, faces, home = (YD, fd, 3) if high else (YU, fu, 0)
            source = find(b, 2 if high else 3, 16 if high else 8)

            def tile(where, i, part):
                src, p = where
                return pltpu.roll(faces[src, i, pl.ds(8 * part, 8), :], (32 * (home + 4 - p)) & 127, 1)

            edge = (lane >= 96) if high else (lane < 32)
            for c in range(1, 19):
                step_x, step_y, _ = VELOCITY[c]
                in_y = step_y == flow
                if in_y:
                    i = comps.index(c)
                    tiles = [tile(source, i, part) for part in range(4)]
                    if step_x == 1:
                        near = [tile(corners[1, step_y], i, 3)] + tiles
                        near = [pltpu.roll(t, 1, 0) for t in near]
                        tiles = [jnp.where(sub == 0, near[q], near[q + 1]) for q in range(4)]
                    elif step_x == -1:
                        near = tiles + [tile(corners[-1, step_y], i, 0)]
                        near = [pltpu.roll(t, 7, 0) for t in near]
                        tiles = [jnp.where(sub == 7, near[q + 1], near[q]) for q in range(4)]
                for part in range(4):
                    in_x = (step_x == 1 and part == 0) or (step_x == -1 and part == 3)
                    if not in_y and not in_x:
                        continue
                    ref = at(c, part, high)
                    now = ref[...]
                    if in_x:
                        k = (XP if step_x == 1 else XM).index(c)
                        now = with_row(now, xs[step_x], step_x, k, 7 * high)
                    if in_y:
                        now = jnp.where(edge, tiles[part], now)
                    ref[...] = now

    xs = {1: find(leaver, 1, 0), -1: find(leaver, 0, 0)}
    patch_columns(leaver, xs, lambda c, part, high: got.at[19 * 7 * high + c, pl.ds(8 * part, 8), :])
    for step_x, comps in ((1, XP), (-1, XM)):
        for k, c in enumerate(comps):
            for v in range(1, 7):
                ref = got.at[19 * v + c, pl.ds(0 if step_x == 1 else 24, 8), :]
                ref[...] = with_row(ref[...], xs[step_x], step_x, k, v)

    def send(v):
        return pltpu.make_async_copy(
            got.at[pl.ds(19 * v, 19)], out.at[leaver, :, :, pl.ds(128 * v, 128)], got_sem.at[v]
        )

    for v in range(8):
        send(v).start()

    def send_sides(j):
        b = staying(j, leaver)
        return [
            pltpu.make_async_copy(
                streamed.at[j, :, 1 + 7 * high, pl.ds(8, 32), :],
                out.at[b, :, :, pl.ds(896 * high, 128)],
                side_sem.at[j, high],
            )
            for high in range(2)
        ] + [
            pltpu.make_async_copy(
                rows.at[j, last, :, pl.ds(7 * last, 1), :],
                out.at[b, pl.ds(1, 14), pl.ds(31 * last, 1), pl.ds(128, 768)],
                row_sem.at[j, last],
            )
            for last in range(2)
        ]

    def finish_block(j, carry):
        b = staying(j, leaver)
        xs = {1: find(b, 1, 0), -1: find(b, 0, 0)}
        patch_columns(b, xs, lambda c, part, high: streamed.at[j, c, 1 + 7 * high, pl.ds(8 + 8 * part, 8), :])
        for last, step_x, comps in ((0, 1, XP), (1, -1, XM)):
            for c in range(1, 15):
                for v in range(1, 7):
                    now = streamed[j, c, v + 1, pl.ds(8 + 24 * last, 8), :]
                    if c in comps:
                        now = with_row(now, xs[step_x], step_x, comps.index(c), v)
                    rows[j, last, c - 1, :, pl.ds(128 * (v - 1), 128)] = now
        for cp in send_sides(j):
            cp.start()
        return carry

    lax.fori_loop(0, 3, finish_block, 0)
    for j in range(3):
        for cp in send_sides(j):
            cp.wait()
    for v in range(8):
        send(v).wait()


def route(shift, cross):
    count = lax.axis_size("gx") * lax.axis_size("gy")
    return [(d, ((d + shift) % count) ^ cross) for d in range(count)]


def on_device(populations, solid_share, migration, neighbours):
    populations = pltpu.with_memory_space_constraint(populations, pltpu.HBM)
    solid_share = pltpu.with_memory_space_constraint(solid_share, pltpu.HBM)
    migration = pltpu.with_memory_space_constraint(migration, pltpu.HBM)
    neighbours = pltpu.with_memory_space_constraint(neighbours, pltpu.HBM)
    dma = pltpu.SemaphoreType.DMA
    mib = 2**20
    stream_shape = pltpu.VMEM((3, 19, 10, 48, 128), F32)
    mate_shape = pltpu.VMEM((MATE, 32, 128), F32)
    halo_shape = pltpu.VMEM((6, 32, 128), F32)
    out_shape = jax.ShapeDtypeStruct((4, 19, 32, 1024), F32)
    raw, streamed, mate, rise, fall = pl.pallas_call(
        first_kernel,
        name="faces_and_leaver",
        out_shape=(pltpu.VMEM((4, 20, 32, 1024), F32), stream_shape, mate_shape, halo_shape, halo_shape),
        in_specs=[SMEM, HBM, HBM],
        out_specs=(VMEM,) * 5,
        scratch_shapes=[pltpu.VMEM((19, 10, 48, 128), F32), dma((4,)), dma((4,)), dma((8,))],
        compiler_params=pltpu.CompilerParams(vmem_limit_bytes=LIMITS[0] * mib),
        cost_estimate=pl.CostEstimate(flops=20_000_000, bytes_accessed=12_000_000, transcendentals=0),
    )(migration, populations, solid_share)

    axes = ("gx", "gy")
    low_a = lax.ppermute(rise, axes, route(2, 0))
    low_b = lax.ppermute(rise, axes, route(2, 1))
    high_a = lax.ppermute(fall, axes, route(-2, 0))
    high_b = lax.ppermute(fall, axes, route(-2, 1))
    got = lax.ppermute(mate, axes, route(0, 1))

    out, streamed = pl.pallas_call(
        second_kernel,
        name="staying_blocks",
        out_shape=(out_shape, stream_shape),
        in_specs=[SMEM, VMEM, VMEM, VMEM],
        out_specs=(HBM, VMEM),
        input_output_aliases={2: 1},
        scratch_shapes=[dma((3, 8))],
        compiler_params=pltpu.CompilerParams(vmem_limit_bytes=LIMITS[1] * mib),
        cost_estimate=pl.CostEstimate(flops=30_000_000, bytes_accessed=16_000_000, transcendentals=0),
    )(migration, raw, streamed, rise)

    out, _, _ = pl.pallas_call(
        third_kernel,
        name="patch_boundaries",
        out_shape=(out_shape, mate_shape, stream_shape),
        in_specs=[SMEM, SMEM] + [VMEM] * 7 + [HBM],
        out_specs=(HBM, VMEM, VMEM),
        input_output_aliases={9: 0, 7: 1, 8: 2},
        scratch_shapes=[
            pltpu.VMEM((2, 10, 32, 128), F32),
            pltpu.VMEM((4, 5, 32, 128), F32),
            pltpu.VMEM((4, 5, 32, 128), F32),
            pltpu.VMEM((3, 2, 14, 8, 768), F32),
            pltpu.SMEM((5, 128), F32),
            pltpu.SMEM((24,), jnp.int32),
            dma((5,)), dma((8,)), dma((3, 2)), dma((3, 2)),
        ],
        compiler_params=pltpu.CompilerParams(vmem_limit_bytes=LIMITS[2] * mib),
        cost_estimate=pl.CostEstimate(flops=1_000_000, bytes_accessed=8_000_000, transcendentals=0),
    )(neighbours, migration, mate, low_a, low_b, high_a, high_b, got, streamed, out)
    return out


def solution(mesh):
    return jax.shard_map(
        on_device,
        mesh=mesh,
        in_specs=(
            P(("gx", "gy"), None, None, None),
            P(("gx", "gy"), None, None),
            P(("gx", "gy")),
            P(("gx", "gy"), None),
        ),
        out_specs=P(("gx", "gy"), None, None, None),
        check_vma=False,
    )
```

```python
import functools

import jax
import jax.numpy as jnp
from jax import lax
from jax.experimental import pallas as pl
from jax.experimental.pallas import tpu as pltpu
from jax.sharding import PartitionSpec as P

VELOCITY = [
    (0, 0, 0), (1, 0, 0), (-1, 0, 0), (0, 1, 0), (0, -1, 0), (0, 0, 1), (0, 0, -1),
    (1, 1, 0), (-1, -1, 0), (1, -1, 0), (-1, 1, 0), (1, 0, 1), (-1, 0, -1), (1, 0, -1),
    (-1, 0, 1), (0, 1, 1), (0, -1, -1), (0, 1, -1), (0, -1, 1),
]
XP = [1, 7, 9, 11, 13]
XM = [2, 8, 10, 12, 14]
YU = [3, 7, 10, 15, 17]
YD = [4, 8, 9, 16, 18]
F32 = jnp.float32
HBM = pl.BlockSpec(memory_space=pltpu.HBM)
VMEM = pl.BlockSpec(memory_space=pltpu.VMEM)
SMEM = pl.BlockSpec(memory_space=pltpu.SMEM)
FX_AT, FU_AT, FD_AT, TAG_AT, MATE = 152, 162, 167, 172, 173
HALO = 21


def collide(f, share):
    q = 1.0 - share
    s = [None] * 19
    d = [None] * 19
    for i in range(1, 19, 2):
        s[i] = f[i] + f[i + 1]
        d[i] = f[i] - f[i + 1]
    dxy, exy = s[7] + s[9], s[7] - s[9]
    dxz, exz = s[11] + s[13], s[11] - s[13]
    dyz, eyz = s[15] + s[17], s[15] - s[17]
    sx = (s[1] + s[3]) + s[5]
    sd = (dxy + dxz) + dyz
    rho = (f[0] + sx) + sd
    axy, bxy = d[7] + d[9], d[7] - d[9]
    axz, bxz = d[11] + d[13], d[11] - d[13]
    ayz, byz = d[15] + d[17], d[15] - d[17]
    tx, ty, tz = axy + axz, bxy + ayz, bxz + byz
    jx, jy, jz = d[1] + tx, d[3] + ty, d[5] + tz
    r = pl.reciprocal(rho, approx=True)
    r = r * (2.0 - rho * r)
    vx, vy, vz = jx * r, jy * r, jz * r
    ux, uy, uz = jx * vx, jy * vy, jz * vz
    j2 = (ux + uy) + uz
    iso_a = (-173.0 / 1800.0) * f[0] + (-4.0 / 45.0) * sx + ((-29.0 / 600.0) * sd + (197.0 / 1800.0) * j2)
    iso_d = (-23.0 / 900.0) * f[0] + (-1.0 / 36.0) * sx + ((-19.0 / 300.0) * sd + (-103.0 / 900.0) * j2)
    iso_0 = (53.0 / 60.0) * f[0] + (-7.0 / 15.0) * sx + ((-5.0 / 12.0) * sd + 0.65 * j2)

    def axis_even(x, dd, u):
        return q * ((11.0 / 15.0) * x + (-1.0 / 30.0) * dd + ((-23.0 / 60.0) * u + iso_a))

    def plane_even(x, dd, u):
        return q * ((-1.0 / 30.0) * x + (23.0 / 60.0) * dd + ((5.0 / 24.0) * u + iso_d))

    q4 = 0.4 * q
    q2 = 0.2 * q
    qm = 0.2475 * q
    ex, ey, ez = axis_even(s[1], dyz, ux), axis_even(s[3], dxz, uy), axis_even(s[5], dxy, uz)
    pyz, pxz, pxy = plane_even(s[1], dyz, ux), plane_even(s[3], dxz, uy), plane_even(s[5], dxy, uz)
    hxy, hxz, hyz = q4 * (exy - jx * vy), q4 * (exz - jx * vz), q4 * (eyz - jy * vz)
    hx = q2 * ((d[1] + d[1]) - tx)
    hy = q2 * ((d[3] + d[3]) - ty)
    hz = q2 * ((d[5] + d[5]) - tz)
    gx, gy, gz = 0.25 * hx, 0.25 * hy, 0.25 * hz
    mx, my, mz = qm * (axy - axz), qm * (ayz - bxy), qm * (bxz - byz)
    axy_o, bxy_o = mx - gx, -(my + gy)
    axz_o, bxz_o = -(mx + gx), mz - gz
    ayz_o, byz_o = my - gy, -(mz + gz)
    odd = {
        1: hx, 3: hy, 5: hz,
        7: axy_o + bxy_o, 9: axy_o - bxy_o,
        11: axz_o + bxz_o, 13: axz_o - bxz_o,
        15: ayz_o + byz_o, 17: ayz_o - byz_o,
    }
    even = {
        1: ex, 3: ey, 5: ez,
        7: pxy + hxy, 9: pxy - hxy,
        11: pxz + hxz, 13: pxz - hxz,
        15: pyz + hyz, 17: pyz - hyz,
    }
    post = [None] * 19
    post[0] = f[0] - q * iso_0
    for i in range(1, 19, 2):
        w = odd[i] + share * d[i]
        post[i] = (f[i] - even[i]) - w
        post[i + 1] = (f[i + 1] - even[i]) + w
    return post


def lane_tables():
    lane = lax.broadcasted_iota(jnp.int32, (8, 128), 1)
    tables = {}
    for step_y in (-1, 0, 1):
        for step_z in (-1, 1):
            tables[step_y, step_z] = ((lane - 32 * step_y) & 96) | ((lane - step_z) & 31)
    return lane, tables


def turn(x, step_y, step_z, tables):
    if step_z:
        return jnp.take_along_axis(x, tables[step_y, step_z], axis=1)
    return pltpu.roll(x, (32 * step_y) % 128, 1) if step_y else x


ORDER = [5, 11, 14, 6, 12, 13, 15, 17, 16, 18, 3, 7, 10, 4, 8, 9]


def collide_part(source, column, part, stage, result):
    at = pl.ds(pl.multiple_of(column * 128, 128), 128)
    rows = pl.ds(8 * part, 8)
    post = collide([source[c, rows, at] for c in range(19)], source[19, rows, at])
    for c in range(3):
        result[c, column + 1, pl.ds(8 + 8 * part + VELOCITY[c][0], 8), :] = post[c]
    for c in range(3, 19):
        stage[c - 3, rows, :] = post[c]


def turn_all(stage, column, result, lanes_of):
    lane, tables = lanes_of
    for c in ORDER:
        step_x, step_y, step_z = VELOCITY[c]
        out = (lane < 32) if step_y == 1 else (lane >= 96)
        for part in range(4):
            value = turn(stage[c - 3, pl.ds(8 * part, 8), :], step_y, step_z, tables)
            to = pl.ds(8 + 8 * part + step_x, 8)
            if step_y == 0:
                result[c, column + 1, to, :] = value
            else:
                pltpu.store(result.at[c, column + 1, to, :], value, mask=jnp.logical_not(out))
                pltpu.store(result.at[c, column + 1 + step_y, to, :], value, mask=out)


def process(source, result, stage, lanes_of, after):
    def one(v, carry):
        for part in range(4):
            collide_part(source, v, part, stage, result)
        turn_all(stage, v, result, lanes_of)
        after(v)
        return carry

    lax.fori_loop(0, 8, one, 0)


def device_index():
    return lax.axis_index("gx") * lax.axis_size("gy") + lax.axis_index("gy")


def leaver_of(migration):
    base = device_index() * 4
    leaver = jnp.int32(0)
    moving = jnp.bool_(False)
    for b in (3, 2, 1, 0):
        away = migration[b] != base + b
        leaver = jnp.where(away, b, leaver)
        moving = jnp.logical_or(moving, away)
    return leaver, moving


def staying(j, leaver):
    return j + (j >= leaver).astype(jnp.int32)


def early_blocks():
    return jnp.where(device_index() < 2, 3, 2).astype(jnp.int32)


def block_at(p, leaver):
    return jnp.where(p == 0, leaver, staying(p - 1, leaver))


def first_kernel(migration, neighbours, pop, share, raw, streamed, mate, stage, pop_sem, share_sem, mate_sem):
    lanes_of = lane_tables()
    lane, tables = lanes_of
    segment = lane >> 5
    sub = lax.broadcasted_iota(jnp.int32, (8, 128), 0)
    leaver, _ = leaver_of(migration)

    def load(p):
        b = block_at(p, leaver)
        return (
            pltpu.make_async_copy(pop.at[b], raw.at[p, pl.ds(0, 19)], pop_sem.at[p]),
            pltpu.make_async_copy(share.at[b], raw.at[p, 19], share_sem.at[p]),
        )

    for p in range(4):
        for cp in load(p):
            cp.start()

    pair = (device_index() >> 1) << 3
    tag = jnp.zeros((8, 128), F32)
    for p in range(4):
        slot = migration[block_at(p, leaver)]
        above = (((neighbours[p, 2] >> 3) << 3) != pair).astype(jnp.int32)
        value = jnp.where(sub == 0, jnp.full((8, 128), slot, jnp.int32), jnp.full((8, 128), above, jnp.int32))
        tag = jnp.where(segment == p, value.astype(F32), tag)
    mate[TAG_AT, pl.ds(0, 8), :] = tag

    def faces(p):
        mine = segment == p
        for part in range(4):
            rows = pl.ds(8 * part, 8)

            def ends(c):
                return jnp.where(lane < 64, raw[p, c, rows, pl.ds(0, 128)], raw[p, c, rows, pl.ds(896, 128)])

            post = collide([ends(c) for c in range(19)], ends(19))
            for comps, at, shift in ((YU, FU_AT, 32 * p + 32), (YD, FD_AT, 32 * p)):
                for i, c in enumerate(comps):
                    value = pltpu.roll(turn(post[c], 0, VELOCITY[c][2], tables), shift & 127, 1)
                    pltpu.store(mate.at[at + i, rows, :], value, mask=mine)

        for end, comps in ((0, XP), (1, XM)):

            def packed(c):
                got = None
                for v in range(8):
                    x = raw[p, c, pl.ds(24 - 24 * end, 8), pl.ds(128 * v, 128)]
                    shift = (v + 1 - end) % 8
                    x = pltpu.roll(x, shift, 0) if shift else x
                    got = x if got is None else jnp.where(sub == v, x, got)
                return got

            post = collide([packed(c) for c in range(19)], packed(19))
            for i, c in enumerate(comps):
                _, step_y, step_z = VELOCITY[c]
                value = turn(post[c], step_y, step_z, tables)
                if step_y:
                    out = (lane < 32) if step_y == 1 else (lane >= 96)
                    value = jnp.where(out, pltpu.roll(value, step_y % 8, 0), value)
                mate[FX_AT + 5 * end + i, pl.ds(pl.multiple_of(8 * p, 8), 8), :] = value

    def hand(v):
        return pltpu.make_async_copy(
            streamed.at[0, :, v + 1, pl.ds(8, 32), :], mate.at[pl.ds(19 * v, 19)], mate_sem.at[v]
        )

    def work(p, carry):
        for cp in load(p):
            cp.wait()
        faces(p)

        @pl.when(p == 0)
        def _():
            def after(v):
                @pl.when(v > 0)
                def _():
                    hand(v - 1).start()

            process(raw.at[0], streamed.at[0], stage, lanes_of, after)
            hand(7).start()

        return carry

    lax.fori_loop(0, 4, work, 0)
    for v in range(8):
        hand(v).wait()


def staying_kernel(late, migration, raw, held, after, *refs):
    out, streamed, stage, out_sem = refs[-4:]
    lanes_of = lane_tables()
    leaver, _ = leaver_of(migration)

    def send(p, v):
        return pltpu.make_async_copy(
            streamed.at[p, :, v + 1, pl.ds(8, 32), :],
            out.at[block_at(p, leaver), :, :, pl.ds(pl.multiple_of(v * 128, 128), 128)],
            out_sem.at[p - 1, v],
        )

    def block(p, carry):
        def after(v):
            @pl.when(v > 1)
            def _():
                send(p, v - 1).start()

        process(raw.at[p], streamed.at[p], stage, lanes_of, after)
        return carry

    def finish(p, carry):
        for v in range(1, 7):
            send(p, v).wait()
        return carry

    middle = early_blocks() + 1
    low, high = (middle, 4) if late else (1, middle)
    lax.fori_loop(low, high, block, 0)
    lax.fori_loop(low, high, finish, 0)


def select_kernel(migration, mine, got, after, rise, fall, faces, tags, table, places, tag_sem):
    del after
    leaver, _ = leaver_of(migration)
    lane = lax.broadcasted_iota(jnp.int32, (8, 128), 1)
    segment = lane >> 5
    tag_copies = [
        pltpu.make_async_copy(ref.at[TAG_AT, pl.ds(0, 2)], tags.at[s], tag_sem.at[s]) for s, ref in enumerate((mine, got))
    ]
    for cp in tag_copies:
        cp.start()
    for s, ref in enumerate((mine, got)):
        for high, at in enumerate((FU_AT, FD_AT)):
            faces[s, high] = ref[pl.ds(at, 5)]
    for cp in tag_copies:
        cp.wait()
    for s in range(2):
        for p in range(4):
            table[tags[s, 0, 32 * p].astype(jnp.int32) & 7] = 4 * s + p
    own = (device_index() & 1) * 4
    ups, downs = jnp.int32(0), jnp.int32(0)
    for s in range(2):
        for b in range(4):
            up = tags[s, 1, 32 * b].astype(jnp.int32)
            slot = (own ^ (4 * s)) + b
            places[jnp.where(up == 1, ups, 4 + downs)] = slot
            ups, downs = ups + up, downs + 1 - up
    pair = (device_index() >> 1) << 3
    for high, halo in enumerate((rise, fall)):
        tag = jnp.zeros((8, 128), F32)
        where = []
        for m in range(4):
            slot = places[4 * high + m]
            code = table[slot]
            where.append((code >> 2, code & 3))
            tag = jnp.where(segment == m, jnp.full((8, 128), pair + slot, jnp.int32).astype(F32), tag)
        halo[20] = tag
        for i in range(5):
            for part in range(4):
                got_tile = None
                for m, (src, p) in enumerate(where):
                    x = pltpu.roll(faces[src, high, i, pl.ds(8 * part, 8), :], (32 * (4 + m - p)) & 127, 1)
                    got_tile = x if m == 0 else jnp.where(segment == m, x, got_tile)
                halo[4 * i + part] = got_tile


def third_kernel(neighbours, migration, mine, high, low, got_in, held, out_in,
                 out, got, streamed, fx, fu, fd, rows, tags, table, tag_sem, got_sem, side_sem, row_sem):
    del got_in, held, out_in
    pair = (device_index() >> 1) << 3
    leaver, moving = leaver_of(migration)
    lane = lax.broadcasted_iota(jnp.int32, (8, 128), 1)
    sub = lax.broadcasted_iota(jnp.int32, (8, 128), 0)

    tag_copies = [pltpu.make_async_copy(got.at[TAG_AT, pl.ds(0, 1)], tags.at[pl.ds(0, 1)], tag_sem.at[0])]
    for k, ref in enumerate((low, high)):
        tag_copies.append(pltpu.make_async_copy(ref.at[20, pl.ds(0, 1)], tags.at[pl.ds(k + 1, 1)], tag_sem.at[k + 1]))
    for cp in tag_copies:
        cp.start()

    for s, ref in enumerate((mine, got)):
        fx[s] = ref[pl.ds(FX_AT, 10)]
        fu[s] = ref[pl.ds(FU_AT, 5)]
        fd[s] = ref[pl.ds(FD_AT, 5)]
    for n in range(20):
        fu[2, n // 4, pl.ds(8 * (n % 4), 8), :] = low[n]
        fd[2, n // 4, pl.ds(8 * (n % 4), 8), :] = high[n]

    @pl.when(jnp.logical_not(moving))
    def _():
        def keep(n, carry):
            got[n] = mine[n]
            return carry

        lax.fori_loop(0, FX_AT, keep, 0)

    for cp in tag_copies:
        cp.wait()
    for p in range(4):
        table[migration[leaver if p == 0 else staying(p - 1, leaver)] & 7] = p
        for k, (start, source) in enumerate(((0, 1), (8, 2), (16, 2))):
            table[start + (tags[k, 32 * p].astype(jnp.int32) & 7)] = 4 * source + p

    def find(b, k, beside):
        slot = neighbours[b, k]
        code = table[(slot & 7) + jnp.where((slot >> 3) << 3 == pair, 0, beside)]
        return code >> 2, code & 3

    def with_row(now, where, step_x, k, column):
        src, p = where
        home, start = (0, 0) if step_x == 1 else (7, 5)
        x = fx[src, start + k, pl.ds(pl.multiple_of(8 * p, 8), 8), :]
        return jnp.where(sub == home, pltpu.roll(x, (home - column) % 8, 0), now)

    def patch_columns(b, xs, at):
        corners = {
            (1, 1): find(b, 5, 8), (-1, 1): find(b, 6, 8),
            (-1, -1): find(b, 4, 16), (1, -1): find(b, 7, 16),
        }
        for high in (0, 1):
            flow = -1 if high else 1
            comps, faces, home = (YD, fd, 3) if high else (YU, fu, 0)
            source = find(b, 2 if high else 3, 16 if high else 8)

            def tile(where, i, part):
                src, p = where
                return pltpu.roll(faces[src, i, pl.ds(8 * part, 8), :], (32 * (home + 4 - p)) & 127, 1)

            edge = (lane >= 96) if high else (lane < 32)
            for c in range(1, 19):
                step_x, step_y, _ = VELOCITY[c]
                in_y = step_y == flow
                if in_y:
                    i = comps.index(c)
                    tiles = [tile(source, i, part) for part in range(4)]
                    if step_x == 1:
                        near = [tile(corners[1, step_y], i, 3)] + tiles
                        near = [pltpu.roll(t, 1, 0) for t in near]
                        tiles = [jnp.where(sub == 0, near[q], near[q + 1]) for q in range(4)]
                    elif step_x == -1:
                        near = tiles + [tile(corners[-1, step_y], i, 0)]
                        near = [pltpu.roll(t, 7, 0) for t in near]
                        tiles = [jnp.where(sub == 7, near[q + 1], near[q]) for q in range(4)]
                for part in range(4):
                    in_x = (step_x == 1 and part == 0) or (step_x == -1 and part == 3)
                    if not in_y and not in_x:
                        continue
                    ref = at(c, part, high)
                    now = ref[...]
                    if in_x:
                        k = (XP if step_x == 1 else XM).index(c)
                        now = with_row(now, xs[step_x], step_x, k, 7 * high)
                    if in_y:
                        now = jnp.where(edge, tiles[part], now)
                    ref[...] = now

    xs = {1: find(leaver, 1, 0), -1: find(leaver, 0, 0)}
    patch_columns(leaver, xs, lambda c, part, high: got.at[19 * 7 * high + c, pl.ds(8 * part, 8), :])
    for step_x, comps in ((1, XP), (-1, XM)):
        for k, c in enumerate(comps):
            for v in range(1, 7):
                ref = got.at[19 * v + c, pl.ds(0 if step_x == 1 else 24, 8), :]
                ref[...] = with_row(ref[...], xs[step_x], step_x, k, v)

    def send(v):
        return pltpu.make_async_copy(
            got.at[pl.ds(19 * v, 19)], out.at[leaver, :, :, pl.ds(128 * v, 128)], got_sem.at[v]
        )

    for v in range(8):
        send(v).start()

    def send_sides(j):
        b = staying(j, leaver)
        return [
            pltpu.make_async_copy(
                streamed.at[j + 1, :, 1 + 7 * high, pl.ds(8, 32), :],
                out.at[b, :, :, pl.ds(896 * high, 128)],
                side_sem.at[j, high],
            )
            for high in range(2)
        ] + [
            pltpu.make_async_copy(
                rows.at[j, last, :, pl.ds(7 * last, 1), :],
                out.at[b, pl.ds(1, 14), pl.ds(31 * last, 1), pl.ds(128, 768)],
                row_sem.at[j, last],
            )
            for last in range(2)
        ]

    def finish_block(j, carry):
        b = staying(j, leaver)
        xs = {1: find(b, 1, 0), -1: find(b, 0, 0)}
        patch_columns(b, xs, lambda c, part, high: streamed.at[j + 1, c, 1 + 7 * high, pl.ds(8 + 8 * part, 8), :])
        for last, step_x, comps in ((0, 1, XP), (1, -1, XM)):
            for c in range(1, 15):
                for v in range(1, 7):
                    now = streamed[j + 1, c, v + 1, pl.ds(8 + 24 * last, 8), :]
                    if c in comps:
                        now = with_row(now, xs[step_x], step_x, comps.index(c), v)
                    rows[j, last, c - 1, :, pl.ds(128 * (v - 1), 128)] = now
        for cp in send_sides(j):
            cp.start()
        return carry

    lax.fori_loop(0, 3, finish_block, 0)
    for j in range(3):
        for cp in send_sides(j):
            cp.wait()
    for v in range(8):
        send(v).wait()


def route(shift, cross):
    count = lax.axis_size("gx") * lax.axis_size("gy")
    return [(d, ((d + shift) % count) ^ cross) for d in range(count)]


def on_device(populations, solid_share, migration, neighbours):
    populations = pltpu.with_memory_space_constraint(populations, pltpu.HBM)
    solid_share = pltpu.with_memory_space_constraint(solid_share, pltpu.HBM)
    migration = pltpu.with_memory_space_constraint(migration, pltpu.HBM)
    neighbours = pltpu.with_memory_space_constraint(neighbours, pltpu.HBM)
    dma = pltpu.SemaphoreType.DMA
    mib = 2**20
    stage = pltpu.VMEM((16, 32, 128), F32)
    stream_shape = pltpu.VMEM((4, 19, 10, 48, 128), F32)
    mate_shape = pltpu.VMEM((MATE, 32, 128), F32)
    halo_shape = pltpu.VMEM((HALO, 8, 128), F32)
    out_shape = jax.ShapeDtypeStruct((4, 19, 32, 1024), F32)

    def params(limit):
        return pltpu.CompilerParams(vmem_limit_bytes=limit * mib)

    def cost(flops, data):
        return pl.CostEstimate(flops=flops, bytes_accessed=data, transcendentals=0)

    raw, streamed, mate = pl.pallas_call(
        first_kernel,
        name="faces_and_leaver",
        out_shape=(pltpu.VMEM((4, 20, 32, 1024), F32), stream_shape, mate_shape),
        in_specs=[SMEM, SMEM, HBM, HBM],
        out_specs=(VMEM,) * 3,
        scratch_shapes=[stage, dma((4,)), dma((4,)), dma((8,))],
        compiler_params=params(4),
        cost_estimate=cost(20_000_000, 12_000_000),
    )(migration, neighbours, populations, solid_share)

    axes = ("gx", "gy")
    got = lax.ppermute(mate, axes, route(0, 1))

    out, streamed = pl.pallas_call(
        functools.partial(staying_kernel, False),
        name="early_blocks",
        out_shape=(out_shape, stream_shape),
        in_specs=[SMEM, VMEM, VMEM, VMEM],
        out_specs=(HBM, VMEM),
        input_output_aliases={2: 1},
        scratch_shapes=[stage, dma((3, 8))],
        compiler_params=params(4),
        cost_estimate=cost(30_000_000, 16_000_000),
    )(migration, raw, streamed, mate)

    rise, fall = pl.pallas_call(
        select_kernel,
        name="select_faces",
        out_shape=(halo_shape, halo_shape),
        in_specs=[SMEM, VMEM, VMEM, VMEM],
        out_specs=(VMEM, VMEM),
        scratch_shapes=[
            pltpu.VMEM((2, 2, 5, 32, 128), F32),
            pltpu.SMEM((2, 2, 128), F32),
            pltpu.SMEM((8,), jnp.int32),
            pltpu.SMEM((8,), jnp.int32),
            dma((2,)),
        ],
        compiler_params=params(4),
        cost_estimate=cost(1_000_000, 1_000_000),
    )(migration, mate, got, streamed)
    low = lax.ppermute(rise, axes, route(2, 0))
    high = lax.ppermute(fall, axes, route(-2, 0))

    out, streamed = pl.pallas_call(
        functools.partial(staying_kernel, True),
        name="late_blocks",
        out_shape=(out_shape, stream_shape),
        in_specs=[SMEM, VMEM, VMEM, VMEM, HBM],
        out_specs=(HBM, VMEM),
        input_output_aliases={4: 0, 2: 1},
        scratch_shapes=[stage, dma((3, 8))],
        compiler_params=params(4),
        cost_estimate=cost(30_000_000, 16_000_000),
    )(migration, raw, streamed, rise, out)

    out, _, _ = pl.pallas_call(
        third_kernel,
        name="patch_boundaries",
        out_shape=(out_shape, mate_shape, stream_shape),
        in_specs=[SMEM, SMEM] + [VMEM] * 5 + [HBM],
        out_specs=(HBM, VMEM, VMEM),
        input_output_aliases={7: 0, 5: 1, 6: 2},
        scratch_shapes=[
            pltpu.VMEM((2, 10, 32, 128), F32),
            pltpu.VMEM((3, 5, 32, 128), F32),
            pltpu.VMEM((3, 5, 32, 128), F32),
            pltpu.VMEM((3, 2, 14, 8, 768), F32),
            pltpu.SMEM((3, 128), F32),
            pltpu.SMEM((24,), jnp.int32),
            dma((3,)), dma((8,)), dma((3, 2)), dma((3, 2)),
        ],
        compiler_params=params(8),
        cost_estimate=cost(1_000_000, 8_000_000),
    )(neighbours, migration, mate, high, low, got, streamed, out)
    return out


def solution(mesh):
    return jax.shard_map(
        on_device,
        mesh=mesh,
        in_specs=(
            P(("gx", "gy"), None, None, None),
            P(("gx", "gy"), None, None),
            P(("gx", "gy")),
            P(("gx", "gy"), None),
        ),
        out_specs=P(("gx", "gy"), None, None, None),
        check_vma=False,
    )
```

```python
import functools

import jax
import jax.numpy as jnp
from jax import lax
from jax.experimental import pallas as pl
from jax.experimental.pallas import tpu as pltpu
from jax.sharding import PartitionSpec as P

VELOCITY = [
    (0, 0, 0), (1, 0, 0), (-1, 0, 0), (0, 1, 0), (0, -1, 0), (0, 0, 1), (0, 0, -1),
    (1, 1, 0), (-1, -1, 0), (1, -1, 0), (-1, 1, 0), (1, 0, 1), (-1, 0, -1), (1, 0, -1),
    (-1, 0, 1), (0, 1, 1), (0, -1, -1), (0, 1, -1), (0, -1, 1),
]
XP = [1, 7, 9, 11, 13]
XM = [2, 8, 10, 12, 14]
YU = [3, 7, 10, 15, 17]
YD = [4, 8, 9, 16, 18]
F32 = jnp.float32
HBM = pl.BlockSpec(memory_space=pltpu.HBM)
VMEM = pl.BlockSpec(memory_space=pltpu.VMEM)
SMEM = pl.BlockSpec(memory_space=pltpu.SMEM)
FX_AT, FU_AT, FD_AT, TAG_AT, MATE = 152, 162, 167, 172, 173
HALO = 21


def collide(f, share):
    q = 1.0 - share
    s = [None] * 19
    d = [None] * 19
    for i in range(1, 19, 2):
        s[i] = f[i] + f[i + 1]
        d[i] = f[i] - f[i + 1]
    dxy, exy = s[7] + s[9], s[7] - s[9]
    dxz, exz = s[11] + s[13], s[11] - s[13]
    dyz, eyz = s[15] + s[17], s[15] - s[17]
    sx = (s[1] + s[3]) + s[5]
    sd = (dxy + dxz) + dyz
    rho = (f[0] + sx) + sd
    axy, bxy = d[7] + d[9], d[7] - d[9]
    axz, bxz = d[11] + d[13], d[11] - d[13]
    ayz, byz = d[15] + d[17], d[15] - d[17]
    tx, ty, tz = axy + axz, bxy + ayz, bxz + byz
    jx, jy, jz = d[1] + tx, d[3] + ty, d[5] + tz
    r = pl.reciprocal(rho, approx=True)
    r = r * (2.0 - rho * r)
    vx, vy, vz = jx * r, jy * r, jz * r
    ux, uy, uz = jx * vx, jy * vy, jz * vz
    j2 = (ux + uy) + uz
    iso_a = (-173.0 / 1800.0) * f[0] + (-4.0 / 45.0) * sx + ((-29.0 / 600.0) * sd + (197.0 / 1800.0) * j2)
    iso_d = (-23.0 / 900.0) * f[0] + (-1.0 / 36.0) * sx + ((-19.0 / 300.0) * sd + (-103.0 / 900.0) * j2)
    iso_0 = (53.0 / 60.0) * f[0] + (-7.0 / 15.0) * sx + ((-5.0 / 12.0) * sd + 0.65 * j2)

    def axis_even(x, dd, u):
        return q * ((11.0 / 15.0) * x + (-1.0 / 30.0) * dd + ((-23.0 / 60.0) * u + iso_a))

    def plane_even(x, dd, u):
        return q * ((-1.0 / 30.0) * x + (23.0 / 60.0) * dd + ((5.0 / 24.0) * u + iso_d))

    q4 = 0.4 * q
    q2 = 0.2 * q
    qm = 0.2475 * q
    ex, ey, ez = axis_even(s[1], dyz, ux), axis_even(s[3], dxz, uy), axis_even(s[5], dxy, uz)
    pyz, pxz, pxy = plane_even(s[1], dyz, ux), plane_even(s[3], dxz, uy), plane_even(s[5], dxy, uz)
    hxy, hxz, hyz = q4 * (exy - jx * vy), q4 * (exz - jx * vz), q4 * (eyz - jy * vz)
    hx = q2 * ((d[1] + d[1]) - tx)
    hy = q2 * ((d[3] + d[3]) - ty)
    hz = q2 * ((d[5] + d[5]) - tz)
    gx, gy, gz = 0.25 * hx, 0.25 * hy, 0.25 * hz
    mx, my, mz = qm * (axy - axz), qm * (ayz - bxy), qm * (bxz - byz)
    axy_o, bxy_o = mx - gx, -(my + gy)
    axz_o, bxz_o = -(mx + gx), mz - gz
    ayz_o, byz_o = my - gy, -(mz + gz)
    odd = {
        1: hx, 3: hy, 5: hz,
        7: axy_o + bxy_o, 9: axy_o - bxy_o,
        11: axz_o + bxz_o, 13: axz_o - bxz_o,
        15: ayz_o + byz_o, 17: ayz_o - byz_o,
    }
    even = {
        1: ex, 3: ey, 5: ez,
        7: pxy + hxy, 9: pxy - hxy,
        11: pxz + hxz, 13: pxz - hxz,
        15: pyz + hyz, 17: pyz - hyz,
    }
    post = [None] * 19
    post[0] = f[0] - q * iso_0
    for i in range(1, 19, 2):
        w = odd[i] + share * d[i]
        post[i] = (f[i] - even[i]) - w
        post[i + 1] = (f[i + 1] - even[i]) + w
    return post


def lane_tables():
    lane = lax.broadcasted_iota(jnp.int32, (8, 128), 1)
    tables = {}
    for step_y in (-1, 0, 1):
        for step_z in (-1, 1):
            tables[step_y, step_z] = ((lane - 32 * step_y) & 96) | ((lane - step_z) & 31)
    return lane, tables


def turn(x, step_y, step_z, tables):
    if step_z:
        return jnp.take_along_axis(x, tables[step_y, step_z], axis=1)
    return pltpu.roll(x, (32 * step_y) % 128, 1) if step_y else x


ORDER = [5, 11, 14, 6, 12, 13, 15, 17, 16, 18, 3, 7, 10, 4, 8, 9]


def collide_part(source, column, part, stage, result):
    at = pl.ds(pl.multiple_of(column * 128, 128), 128)
    rows = pl.ds(8 * part, 8)
    post = collide([source[c, rows, at] for c in range(19)], source[19, rows, at])
    for c in range(3):
        result[c, column + 1, pl.ds(8 + 8 * part + VELOCITY[c][0], 8), :] = post[c]
    for c in range(3, 19):
        stage[c - 3, rows, :] = post[c]


def turn_all(stage, column, result, lanes_of):
    lane, tables = lanes_of
    for c in ORDER:
        step_x, step_y, step_z = VELOCITY[c]
        out = (lane < 32) if step_y == 1 else (lane >= 96)
        for part in range(4):
            value = turn(stage[c - 3, pl.ds(8 * part, 8), :], step_y, step_z, tables)
            to = pl.ds(8 + 8 * part + step_x, 8)
            if step_y == 0:
                result[c, column + 1, to, :] = value
            else:
                pltpu.store(result.at[c, column + 1, to, :], value, mask=jnp.logical_not(out))
                pltpu.store(result.at[c, column + 1 + step_y, to, :], value, mask=out)


def process(source, result, stage, lanes_of, after):
    def one(v, carry):
        for part in range(4):
            collide_part(source, v, part, stage, result)
        turn_all(stage, v, result, lanes_of)
        after(v)
        return carry

    lax.fori_loop(0, 8, one, 0)


def device_index():
    return lax.axis_index("gx") * lax.axis_size("gy") + lax.axis_index("gy")


def leaver_of(migration):
    base = device_index() * 4
    leaver = jnp.int32(0)
    moving = jnp.bool_(False)
    for b in (3, 2, 1, 0):
        away = migration[b] != base + b
        leaver = jnp.where(away, b, leaver)
        moving = jnp.logical_or(moving, away)
    return leaver, moving


def staying(j, leaver):
    return j + (j >= leaver).astype(jnp.int32)


def early_blocks():
    return jnp.where((device_index() >> 1) & 3 == 0, 3, 2).astype(jnp.int32)


def block_at(p, leaver):
    return jnp.where(p == 0, leaver, staying(p - 1, leaver))


def first_kernel(migration, neighbours, pop, share, raw, mate, leaving, stage, pop_sem, share_sem, mate_sem):
    lanes_of = lane_tables()
    lane, tables = lanes_of
    segment = lane >> 5
    sub = lax.broadcasted_iota(jnp.int32, (8, 128), 0)
    leaver, _ = leaver_of(migration)

    def load(p):
        b = block_at(p, leaver)
        return (
            pltpu.make_async_copy(pop.at[b], raw.at[p, pl.ds(0, 19)], pop_sem.at[p]),
            pltpu.make_async_copy(share.at[b], raw.at[p, 19], share_sem.at[p]),
        )

    for p in range(4):
        for cp in load(p):
            cp.start()

    pair = (device_index() >> 1) << 3
    tag = jnp.zeros((8, 128), F32)
    for p in range(4):
        slot = migration[block_at(p, leaver)]
        above = (((neighbours[p, 2] >> 3) << 3) != pair).astype(jnp.int32)
        value = jnp.where(sub == 0, jnp.full((8, 128), slot, jnp.int32), jnp.full((8, 128), above, jnp.int32))
        tag = jnp.where(segment == p, value.astype(F32), tag)
    mate[TAG_AT, pl.ds(0, 8), :] = tag

    def faces(p):
        mine = segment == p
        for part in range(4):
            rows = pl.ds(8 * part, 8)

            def ends(c):
                return jnp.where(lane < 64, raw[p, c, rows, pl.ds(0, 128)], raw[p, c, rows, pl.ds(896, 128)])

            post = collide([ends(c) for c in range(19)], ends(19))
            for comps, at, shift in ((YU, FU_AT, 32 * p + 32), (YD, FD_AT, 32 * p)):
                for i, c in enumerate(comps):
                    value = pltpu.roll(turn(post[c], 0, VELOCITY[c][2], tables), shift & 127, 1)
                    pltpu.store(mate.at[at + i, rows, :], value, mask=mine)

        for end, comps in ((0, XP), (1, XM)):

            def packed(c):
                got = None
                for v in range(8):
                    x = raw[p, c, pl.ds(24 - 24 * end, 8), pl.ds(128 * v, 128)]
                    shift = (v + 1 - end) % 8
                    x = pltpu.roll(x, shift, 0) if shift else x
                    got = x if got is None else jnp.where(sub == v, x, got)
                return got

            post = collide([packed(c) for c in range(19)], packed(19))
            for i, c in enumerate(comps):
                _, step_y, step_z = VELOCITY[c]
                value = turn(post[c], step_y, step_z, tables)
                if step_y:
                    out = (lane < 32) if step_y == 1 else (lane >= 96)
                    value = jnp.where(out, pltpu.roll(value, step_y % 8, 0), value)
                mate[FX_AT + 5 * end + i, pl.ds(pl.multiple_of(8 * p, 8), 8), :] = value

    def hand(v):
        return pltpu.make_async_copy(
            leaving.at[:, v + 1, pl.ds(8, 32), :], mate.at[pl.ds(19 * v, 19)], mate_sem.at[v]
        )

    def work(p, carry):
        for cp in load(p):
            cp.wait()
        faces(p)

        @pl.when(p == 0)
        def _():
            def after(v):
                @pl.when(v > 0)
                def _():
                    hand(v - 1).start()

            process(raw.at[0], leaving, stage, lanes_of, after)
            hand(7).start()

        return carry

    lax.fori_loop(0, 4, work, 0)
    for v in range(8):
        hand(v).wait()


def column_send(streamed, out, out_sem, leaver, p, v):
    return pltpu.make_async_copy(
        streamed.at[p - 1, :, v + 1, pl.ds(8, 32), :],
        out.at[block_at(p, leaver), :, :, pl.ds(pl.multiple_of(v * 128, 128), 128)],
        out_sem.at[p - 1, v],
    )


def early_kernel(migration, raw, after, out, streamed, stage, out_sem):
    del after
    lanes_of = lane_tables()
    leaver, _ = leaver_of(migration)
    send = functools.partial(column_send, streamed, out, out_sem, leaver)

    def block(p, carry):
        def after_column(v):
            @pl.when(v > 1)
            def _():
                send(p, v - 1).start()

        process(raw.at[p], streamed.at[p - 1], stage, lanes_of, after_column)
        return carry

    def finish(p, carry):
        for v in range(1, 7):
            send(p, v).wait()
        return carry

    end = early_blocks() + 1
    lax.fori_loop(1, end, block, 0)
    lax.fori_loop(1, end, finish, 0)


def late_kernel(neighbours, migration, raw, held, mine, got_in, after, out_in, out, streamed, got,
                stage, fx, rows, tags, table, tag_sem, out_sem, got_sem, row_sem):
    del held, got_in, after, out_in
    lanes_of = lane_tables()
    leaver, moving = leaver_of(migration)
    sub = lax.broadcasted_iota(jnp.int32, (8, 128), 0)
    send = functools.partial(column_send, streamed, out, out_sem, leaver)
    tag_copy = pltpu.make_async_copy(got.at[TAG_AT, pl.ds(0, 1)], tags, tag_sem)
    tag_copy.start()
    for s, ref in enumerate((mine, got)):
        fx[s] = ref[pl.ds(FX_AT, 10)]

    @pl.when(jnp.logical_not(moving))
    def _():
        def keep(n, carry):
            got[n] = mine[n]
            return carry

        lax.fori_loop(0, FX_AT, keep, 0)

    tag_copy.wait()
    for p in range(4):
        table[migration[block_at(p, leaver)] & 7] = p
        table[tags[0, 32 * p].astype(jnp.int32) & 7] = 4 + p

    def incoming(b):
        found = {}
        for step_x, k in ((1, 1), (-1, 0)):
            code = table[neighbours[b, k] & 7]
            found[step_x] = (code >> 2, code & 3)
        return found

    def with_row(now, where, step_x, k, column):
        src, p = where
        home, start = (0, 0) if step_x == 1 else (7, 5)
        x = fx[src, start + k, pl.ds(pl.multiple_of(8 * p, 8), 8), :]
        return jnp.where(sub == home, pltpu.roll(x, (home - column) & 7, 0), now)

    def patch_column(xs, v, at):
        for step_x, comps in ((1, XP), (-1, XM)):
            for k, c in enumerate(comps):
                ref = at(c, 0 if step_x == 1 else 24)
                ref[...] = with_row(ref[...], xs[step_x], step_x, k, v)

    def streamed_at(p, v):
        return lambda c, row: streamed.at[p - 1, c, v + 1, pl.ds(8 + row, 8), :]

    xs = incoming(leaver)

    def arrived(v):
        return pltpu.make_async_copy(
            got.at[pl.ds(19 * v, 19)], out.at[leaver, :, :, pl.ds(128 * v, 128)], got_sem.at[v]
        )

    for v in range(8):
        patch_column(xs, v, lambda c, row: got.at[19 * v + c, pl.ds(row, 8), :])
        if 0 < v < 7:
            arrived(v).start()

    def send_rows(p):
        return [
            pltpu.make_async_copy(
                rows.at[p - 1, last, :, pl.ds(7 * last, 1), :],
                out.at[block_at(p, leaver), pl.ds(1, 14), pl.ds(31 * last, 1), pl.ds(128, 768)],
                row_sem.at[p - 1, last],
            )
            for last in range(2)
        ]

    def written(p, carry):
        xs = incoming(block_at(p, leaver))
        for last, step_x, comps in ((0, 1, XP), (1, -1, XM)):
            for c in range(1, 15):
                for v in range(1, 7):
                    now = streamed[p - 1, c, v + 1, pl.ds(8 + 24 * last, 8), :]
                    if c in comps:
                        now = with_row(now, xs[step_x], step_x, comps.index(c), v)
                    rows[p - 1, last, c - 1, :, pl.ds(128 * (v - 1), 128)] = now
        for cp in send_rows(p):
            cp.start()
        for v in (0, 7):
            patch_column(xs, v, streamed_at(p, v))
        return carry

    def remaining(p, carry):
        xs = incoming(block_at(p, leaver))

        def after_column(v):
            @pl.when(v > 0)
            def _():
                patch_column(xs, v - 1, streamed_at(p, v - 1))

            @pl.when(v > 1)
            def _():
                send(p, v - 1).start()

        process(raw.at[p], streamed.at[p - 1], stage, lanes_of, after_column)
        patch_column(xs, 7, streamed_at(p, 7))
        return carry

    def finish(p, carry):
        for v in range(1, 7):
            send(p, v).wait()
        return carry

    def finish_rows(p, carry):
        for cp in send_rows(p):
            cp.wait()
        return carry

    middle = early_blocks() + 1
    lax.fori_loop(1, middle, written, 0)
    lax.fori_loop(middle, 4, remaining, 0)
    lax.fori_loop(1, middle, finish_rows, 0)
    lax.fori_loop(middle, 4, finish, 0)
    for v in range(1, 7):
        arrived(v).wait()


def select_kernel(migration, mine, got, after, rise, fall, faces, tags, table, places, tag_sem):
    del after
    leaver, _ = leaver_of(migration)
    lane = lax.broadcasted_iota(jnp.int32, (8, 128), 1)
    segment = lane >> 5
    tag_copies = [
        pltpu.make_async_copy(ref.at[TAG_AT, pl.ds(0, 2)], tags.at[s], tag_sem.at[s]) for s, ref in enumerate((mine, got))
    ]
    for cp in tag_copies:
        cp.start()
    for s, ref in enumerate((mine, got)):
        for high, at in enumerate((FU_AT, FD_AT)):
            faces[s, high] = ref[pl.ds(at, 5)]
    for cp in tag_copies:
        cp.wait()
    for s in range(2):
        for p in range(4):
            table[tags[s, 0, 32 * p].astype(jnp.int32) & 7] = 4 * s + p
    own = (device_index() & 1) * 4
    ups, downs = jnp.int32(0), jnp.int32(0)
    for s in range(2):
        for b in range(4):
            up = tags[s, 1, 32 * b].astype(jnp.int32)
            slot = (own ^ (4 * s)) + b
            places[jnp.where(up == 1, ups, 4 + downs)] = slot
            ups, downs = ups + up, downs + 1 - up
    pair = (device_index() >> 1) << 3
    for high, halo in enumerate((rise, fall)):
        tag = jnp.zeros((8, 128), F32)
        where = []
        for m in range(4):
            slot = places[4 * high + m]
            code = table[slot]
            where.append((code >> 2, code & 3))
            tag = jnp.where(segment == m, jnp.full((8, 128), pair + slot, jnp.int32).astype(F32), tag)
        halo[20] = tag
        for i in range(5):
            for part in range(4):
                got_tile = None
                for m, (src, p) in enumerate(where):
                    x = pltpu.roll(faces[src, high, i, pl.ds(8 * part, 8), :], (32 * (4 + m - p)) & 127, 1)
                    got_tile = x if m == 0 else jnp.where(segment == m, x, got_tile)
                halo[4 * i + part] = got_tile


def last_kernel(neighbours, migration, mine, low, high, got, streamed_in, out_in,
                out, streamed, fu, fd, columns, tags, table, tag_sem, got_sem, side_sem):
    del streamed_in, out_in
    pair = (device_index() >> 1) << 3
    leaver, _ = leaver_of(migration)
    lane = lax.broadcasted_iota(jnp.int32, (8, 128), 1)
    sub = lax.broadcasted_iota(jnp.int32, (8, 128), 0)

    tag_copies = [
        pltpu.make_async_copy(ref, tags.at[pl.ds(k, 1)], tag_sem.at[k])
        for k, ref in enumerate((got.at[TAG_AT, pl.ds(0, 1)], low.at[20, pl.ds(0, 1)], high.at[20, pl.ds(0, 1)]))
    ]
    for cp in tag_copies:
        cp.start()
    for s, ref in enumerate((mine, got)):
        fu[s] = ref[pl.ds(FU_AT, 5)]
        fd[s] = ref[pl.ds(FD_AT, 5)]
    for n in range(20):
        fu[2, n // 4, pl.ds(8 * (n % 4), 8), :] = low[n]
        fd[2, n // 4, pl.ds(8 * (n % 4), 8), :] = high[n]
    for high_side in range(2):
        columns[high_side] = got[pl.ds(19 * 7 * high_side, 19)]

    for cp in tag_copies:
        cp.wait()
    for p in range(4):
        table[migration[block_at(p, leaver)] & 7] = p
        for k, (start, source) in enumerate(((0, 1), (8, 2), (16, 2))):
            table[start + (tags[k, 32 * p].astype(jnp.int32) & 7)] = 4 * source + p

    def find(b, k, beside):
        slot = neighbours[b, k]
        code = table[(slot & 7) + jnp.where((slot >> 3) << 3 == pair, 0, beside)]
        return code >> 2, code & 3

    def patch_columns(b, at):
        corners = {
            (1, 1): find(b, 5, 8), (-1, 1): find(b, 6, 8),
            (-1, -1): find(b, 4, 16), (1, -1): find(b, 7, 16),
        }
        for upper in (0, 1):
            comps, faces, home = (YD, fd, 3) if upper else (YU, fu, 0)
            source = find(b, 2 if upper else 3, 16 if upper else 8)
            edge = (lane >= 96) if upper else (lane < 32)

            def tile(where, i, part):
                src, p = where
                return pltpu.roll(faces[src, i, pl.ds(8 * part, 8), :], (32 * (home + 4 - p)) & 127, 1)

            for i, c in enumerate(comps):
                step_x, step_y, _ = VELOCITY[c]
                tiles = [tile(source, i, part) for part in range(4)]
                if step_x == 1:
                    near = [tile(corners[1, step_y], i, 3)] + tiles
                    near = [pltpu.roll(t, 1, 0) for t in near]
                    tiles = [jnp.where(sub == 0, near[q], near[q + 1]) for q in range(4)]
                elif step_x == -1:
                    near = tiles + [tile(corners[-1, step_y], i, 0)]
                    near = [pltpu.roll(t, 7, 0) for t in near]
                    tiles = [jnp.where(sub == 7, near[q + 1], near[q]) for q in range(4)]
                for part in range(4):
                    ref = at(c, part, upper)
                    ref[...] = jnp.where(edge, tiles[part], ref[...])

    def send_arrived(upper):
        return pltpu.make_async_copy(
            columns.at[upper], out.at[leaver, :, :, pl.ds(896 * upper, 128)], got_sem.at[upper]
        )

    patch_columns(leaver, lambda c, part, upper: columns.at[upper, c, pl.ds(8 * part, 8), :])
    for upper in range(2):
        send_arrived(upper).start()

    def send_sides(p):
        return [
            pltpu.make_async_copy(
                streamed.at[p - 1, :, 1 + 7 * upper, pl.ds(8, 32), :],
                out.at[block_at(p, leaver), :, :, pl.ds(896 * upper, 128)],
                side_sem.at[p - 1, upper],
            )
            for upper in range(2)
        ]

    def finish_block(p, carry):
        patch_columns(
            block_at(p, leaver),
            lambda c, part, upper: streamed.at[p - 1, c, 1 + 7 * upper, pl.ds(8 + 8 * part, 8), :],
        )
        for cp in send_sides(p):
            cp.start()
        return carry

    lax.fori_loop(1, 4, finish_block, 0)
    for p in range(1, 4):
        for cp in send_sides(p):
            cp.wait()
    for upper in range(2):
        send_arrived(upper).wait()


def route(shift, cross):
    count = lax.axis_size("gx") * lax.axis_size("gy")
    return [(d, ((d + shift) % count) ^ cross) for d in range(count)]


def on_device(populations, solid_share, migration, neighbours):
    populations = pltpu.with_memory_space_constraint(populations, pltpu.HBM)
    solid_share = pltpu.with_memory_space_constraint(solid_share, pltpu.HBM)
    migration = pltpu.with_memory_space_constraint(migration, pltpu.HBM)
    neighbours = pltpu.with_memory_space_constraint(neighbours, pltpu.HBM)
    dma = pltpu.SemaphoreType.DMA
    mib = 2**20
    stage = pltpu.VMEM((16, 32, 128), F32)
    stream_shape = pltpu.VMEM((3, 19, 10, 48, 128), F32)
    mate_shape = pltpu.VMEM((MATE, 32, 128), F32)
    halo_shape = pltpu.VMEM((HALO, 8, 128), F32)
    out_shape = jax.ShapeDtypeStruct((4, 19, 32, 1024), F32)

    def params(limit):
        return pltpu.CompilerParams(vmem_limit_bytes=limit * mib)

    def cost(flops, data):
        return pl.CostEstimate(flops=flops, bytes_accessed=data, transcendentals=0)

    raw, mate = pl.pallas_call(
        first_kernel,
        name="faces_and_leaver",
        out_shape=(pltpu.VMEM((4, 20, 32, 1024), F32), mate_shape),
        in_specs=[SMEM, SMEM, HBM, HBM],
        out_specs=(VMEM,) * 2,
        scratch_shapes=[pltpu.VMEM((19, 10, 48, 128), F32), stage, dma((4,)), dma((4,)), dma((8,))],
        compiler_params=params(8),
        cost_estimate=cost(20_000_000, 12_000_000),
    )(migration, neighbours, populations, solid_share)

    axes = ("gx", "gy")
    got = lax.ppermute(mate, axes, route(0, 1))

    out, streamed = pl.pallas_call(
        early_kernel,
        name="early_blocks",
        out_shape=(out_shape, stream_shape),
        in_specs=[SMEM, VMEM, VMEM],
        out_specs=(HBM, VMEM),
        scratch_shapes=[stage, dma((3, 8))],
        compiler_params=params(4),
        cost_estimate=cost(30_000_000, 16_000_000),
    )(migration, raw, mate)

    rise, fall = pl.pallas_call(
        select_kernel,
        name="select_faces",
        out_shape=(halo_shape, halo_shape),
        in_specs=[SMEM, VMEM, VMEM, VMEM],
        out_specs=(VMEM, VMEM),
        scratch_shapes=[
            pltpu.VMEM((2, 2, 5, 32, 128), F32),
            pltpu.SMEM((2, 2, 128), F32),
            pltpu.SMEM((8,), jnp.int32),
            pltpu.SMEM((8,), jnp.int32),
            dma((2,)),
        ],
        compiler_params=params(4),
        cost_estimate=cost(1_000_000, 1_000_000),
    )(migration, mate, got, streamed)
    high = lax.ppermute(fall, axes, route(-2, 0))
    low = lax.ppermute(rise, axes, route(2, 0))

    out, streamed, got = pl.pallas_call(
        late_kernel,
        name="late_blocks",
        out_shape=(out_shape, stream_shape, mate_shape),
        in_specs=[SMEM, SMEM] + [VMEM] * 5 + [HBM],
        out_specs=(HBM, VMEM, VMEM),
        input_output_aliases={7: 0, 3: 1, 5: 2},
        scratch_shapes=[
            stage,
            pltpu.VMEM((2, 10, 32, 128), F32),
            pltpu.VMEM((3, 2, 14, 8, 768), F32),
            pltpu.SMEM((1, 128), F32),
            pltpu.SMEM((8,), jnp.int32),
            dma, dma((3, 8)), dma((8,)), dma((3, 2)),
        ],
        compiler_params=params(6),
        cost_estimate=cost(30_000_000, 16_000_000),
    )(neighbours, migration, raw, streamed, mate, got, fall, out)

    out, _ = pl.pallas_call(
        last_kernel,
        name="outer_columns",
        out_shape=(out_shape, stream_shape),
        in_specs=[SMEM, SMEM] + [VMEM] * 5 + [HBM],
        out_specs=(HBM, VMEM),
        input_output_aliases={7: 0, 6: 1},
        scratch_shapes=[
            pltpu.VMEM((3, 5, 32, 128), F32),
            pltpu.VMEM((3, 5, 32, 128), F32),
            pltpu.VMEM((2, 19, 32, 128), F32),
            pltpu.SMEM((3, 128), F32),
            pltpu.SMEM((24,), jnp.int32),
            dma((3,)), dma((2,)), dma((3, 2)),
        ],
        compiler_params=params(6),
        cost_estimate=cost(1_000_000, 8_000_000),
    )(neighbours, migration, mate, low, high, got, streamed, out)
    return out


def solution(mesh):
    return jax.shard_map(
        on_device,
        mesh=mesh,
        in_specs=(
            P(("gx", "gy"), None, None, None),
            P(("gx", "gy"), None, None),
            P(("gx", "gy")),
            P(("gx", "gy"), None),
        ),
        out_specs=P(("gx", "gy"), None, None, None),
        check_vma=False,
    )
```

```python
import functools

import jax
import jax.numpy as jnp
from jax import lax
from jax.experimental import pallas as pl
from jax.experimental.pallas import tpu as pltpu
from jax.sharding import PartitionSpec as P

VELOCITY = [
    (0, 0, 0), (1, 0, 0), (-1, 0, 0), (0, 1, 0), (0, -1, 0), (0, 0, 1), (0, 0, -1),
    (1, 1, 0), (-1, -1, 0), (1, -1, 0), (-1, 1, 0), (1, 0, 1), (-1, 0, -1), (1, 0, -1),
    (-1, 0, 1), (0, 1, 1), (0, -1, -1), (0, 1, -1), (0, -1, 1),
]
XP = [1, 7, 9, 11, 13]
XM = [2, 8, 10, 12, 14]
YU = [3, 7, 10, 15, 17]
YD = [4, 8, 9, 16, 18]
F32 = jnp.float32
HBM = pl.BlockSpec(memory_space=pltpu.HBM)
VMEM = pl.BlockSpec(memory_space=pltpu.VMEM)
SMEM = pl.BlockSpec(memory_space=pltpu.SMEM)
FX_AT, FU_AT, FD_AT, TAG_AT, MATE = 152, 162, 167, 172, 173
HALO = 21


def collide(f, share):
    q = 1.0 - share
    s = [None] * 19
    d = [None] * 19
    for i in range(1, 19, 2):
        s[i] = f[i] + f[i + 1]
        d[i] = f[i] - f[i + 1]
    dxy, exy = s[7] + s[9], s[7] - s[9]
    dxz, exz = s[11] + s[13], s[11] - s[13]
    dyz, eyz = s[15] + s[17], s[15] - s[17]
    sx = (s[1] + s[3]) + s[5]
    sd = (dxy + dxz) + dyz
    rho = (f[0] + sx) + sd
    axy, bxy = d[7] + d[9], d[7] - d[9]
    axz, bxz = d[11] + d[13], d[11] - d[13]
    ayz, byz = d[15] + d[17], d[15] - d[17]
    tx, ty, tz = axy + axz, bxy + ayz, bxz + byz
    jx, jy, jz = d[1] + tx, d[3] + ty, d[5] + tz
    r = pl.reciprocal(rho, approx=True)
    r = r * (2.0 - rho * r)
    vx, vy, vz = jx * r, jy * r, jz * r
    ux, uy, uz = jx * vx, jy * vy, jz * vz
    j2 = (ux + uy) + uz
    iso_a = (-173.0 / 1800.0) * f[0] + (-4.0 / 45.0) * sx + ((-29.0 / 600.0) * sd + (197.0 / 1800.0) * j2)
    iso_d = (-23.0 / 900.0) * f[0] + (-1.0 / 36.0) * sx + ((-19.0 / 300.0) * sd + (-103.0 / 900.0) * j2)
    iso_0 = (53.0 / 60.0) * f[0] + (-7.0 / 15.0) * sx + ((-5.0 / 12.0) * sd + 0.65 * j2)

    def axis_even(x, dd, u):
        return q * ((11.0 / 15.0) * x + (-1.0 / 30.0) * dd + ((-23.0 / 60.0) * u + iso_a))

    def plane_even(x, dd, u):
        return q * ((-1.0 / 30.0) * x + (23.0 / 60.0) * dd + ((5.0 / 24.0) * u + iso_d))

    q4 = 0.4 * q
    q2 = 0.2 * q
    qm = 0.2475 * q
    ex, ey, ez = axis_even(s[1], dyz, ux), axis_even(s[3], dxz, uy), axis_even(s[5], dxy, uz)
    pyz, pxz, pxy = plane_even(s[1], dyz, ux), plane_even(s[3], dxz, uy), plane_even(s[5], dxy, uz)
    hxy, hxz, hyz = q4 * (exy - jx * vy), q4 * (exz - jx * vz), q4 * (eyz - jy * vz)
    hx = q2 * ((d[1] + d[1]) - tx)
    hy = q2 * ((d[3] + d[3]) - ty)
    hz = q2 * ((d[5] + d[5]) - tz)
    gx, gy, gz = 0.25 * hx, 0.25 * hy, 0.25 * hz
    mx, my, mz = qm * (axy - axz), qm * (ayz - bxy), qm * (bxz - byz)
    axy_o, bxy_o = mx - gx, -(my + gy)
    axz_o, bxz_o = -(mx + gx), mz - gz
    ayz_o, byz_o = my - gy, -(mz + gz)
    odd = {
        1: hx, 3: hy, 5: hz,
        7: axy_o + bxy_o, 9: axy_o - bxy_o,
        11: axz_o + bxz_o, 13: axz_o - bxz_o,
        15: ayz_o + byz_o, 17: ayz_o - byz_o,
    }
    even = {
        1: ex, 3: ey, 5: ez,
        7: pxy + hxy, 9: pxy - hxy,
        11: pxz + hxz, 13: pxz - hxz,
        15: pyz + hyz, 17: pyz - hyz,
    }
    post = [None] * 19
    post[0] = f[0] - q * iso_0
    for i in range(1, 19, 2):
        w = odd[i] + share * d[i]
        post[i] = (f[i] - even[i]) - w
        post[i + 1] = (f[i + 1] - even[i]) + w
    return post


def lane_tables():
    lane = lax.broadcasted_iota(jnp.int32, (8, 128), 1)
    tables = {}
    for step_y in (-1, 0, 1):
        for step_z in (-1, 1):
            tables[step_y, step_z] = ((lane - 32 * step_y) & 96) | ((lane - step_z) & 31)
    return lane, tables


def turn(x, step_y, step_z, tables):
    if step_z:
        return jnp.take_along_axis(x, tables[step_y, step_z], axis=1)
    return pltpu.roll(x, (32 * step_y) % 128, 1) if step_y else x


ORDER = [5, 11, 14, 6, 12, 13, 15, 17, 16, 18, 3, 7, 10, 4, 8, 9]


def collide_part(source, column, part, stage, result):
    at = pl.ds(pl.multiple_of(column * 128, 128), 128)
    rows = pl.ds(8 * part, 8)
    post = collide([source[c, rows, at] for c in range(19)], source[19, rows, at])
    for c in range(3):
        result[c, column + 1, pl.ds(8 + 8 * part + VELOCITY[c][0], 8), :] = post[c]
    for c in range(3, 19):
        stage[c - 3, rows, :] = post[c]


def turn_all(stage, column, result, lanes_of):
    lane, tables = lanes_of
    for c in ORDER:
        step_x, step_y, step_z = VELOCITY[c]
        out = (lane < 32) if step_y == 1 else (lane >= 96)
        for part in range(4):
            value = turn(stage[c - 3, pl.ds(8 * part, 8), :], step_y, step_z, tables)
            to = pl.ds(8 + 8 * part + step_x, 8)
            if step_y == 0:
                result[c, column + 1, to, :] = value
            else:
                pltpu.store(result.at[c, column + 1, to, :], value, mask=jnp.logical_not(out))
                pltpu.store(result.at[c, column + 1 + step_y, to, :], value, mask=out)


def process(source, result, stage, lanes_of, after):
    def some(i, carry):
        for h in range(4):
            v = 4 * i + h
            for part in range(4):
                collide_part(source, v, part, stage, result)
            turn_all(stage, v, result, lanes_of)
            after(v)
        return carry

    lax.fori_loop(0, 2, some, 0)


def device_index():
    return lax.axis_index("gx") * lax.axis_size("gy") + lax.axis_index("gy")


def leaver_of(migration):
    base = device_index() * 4
    leaver = jnp.int32(0)
    moving = jnp.bool_(False)
    for b in (3, 2, 1, 0):
        away = migration[b] != base + b
        leaver = jnp.where(away, b, leaver)
        moving = jnp.logical_or(moving, away)
    return leaver, moving


def staying(j, leaver):
    return j + (j >= leaver).astype(jnp.int32)


def early_blocks():
    z = (device_index() >> 1) & 3
    return jnp.where(z == 0, 3, jnp.where(z == 3, 1, 2)).astype(jnp.int32)


def block_at(p, leaver):
    return jnp.where(p == 0, leaver, staying(p - 1, leaver))


def first_kernel(migration, neighbours, pop, share, raw, mate, slots, near, leaving, stage, pop_sem, share_sem, mate_sem):
    lanes_of = lane_tables()
    lane, tables = lanes_of
    segment = lane >> 5
    sub = lax.broadcasted_iota(jnp.int32, (8, 128), 0)
    leaver, _ = leaver_of(migration)

    def load(p):
        b = block_at(p, leaver)
        return (
            pltpu.make_async_copy(pop.at[b], raw.at[p, pl.ds(0, 19)], pop_sem.at[p]),
            pltpu.make_async_copy(share.at[b], raw.at[p, 19], share_sem.at[p]),
        )

    for p in range(4):
        for cp in load(p):
            cp.start()
    for b in range(4):
        slots[b] = migration[b]
        for k in range(8):
            near[b, k] = neighbours[b, k]

    pair = (device_index() >> 1) << 3
    tag = jnp.zeros((8, 128), F32)
    for p in range(4):
        slot = migration[block_at(p, leaver)]
        above = (((neighbours[p, 2] >> 3) << 3) != pair).astype(jnp.int32)
        value = jnp.where(sub == 0, jnp.full((8, 128), slot, jnp.int32), jnp.full((8, 128), above, jnp.int32))
        tag = jnp.where(segment == p, value.astype(F32), tag)
    mate[TAG_AT, pl.ds(0, 8), :] = tag

    def faces(p):
        mine = segment == p
        for part in range(4):
            rows = pl.ds(8 * part, 8)

            def ends(c):
                return jnp.where(lane < 64, raw[p, c, rows, pl.ds(0, 128)], raw[p, c, rows, pl.ds(896, 128)])

            post = collide([ends(c) for c in range(19)], ends(19))
            for comps, at, shift in ((YU, FU_AT, 32 * p + 32), (YD, FD_AT, 32 * p)):
                for i, c in enumerate(comps):
                    value = pltpu.roll(turn(post[c], 0, VELOCITY[c][2], tables), shift & 127, 1)
                    pltpu.store(mate.at[at + i, rows, :], value, mask=mine)

        for end, comps in ((0, XP), (1, XM)):

            def packed(c):
                got = None
                for v in range(8):
                    x = raw[p, c, pl.ds(24 - 24 * end, 8), pl.ds(128 * v, 128)]
                    shift = (v + 1 - end) % 8
                    x = pltpu.roll(x, shift, 0) if shift else x
                    got = x if got is None else jnp.where(sub == v, x, got)
                return got

            post = collide([packed(c) for c in range(19)], packed(19))
            for i, c in enumerate(comps):
                _, step_y, step_z = VELOCITY[c]
                value = turn(post[c], step_y, step_z, tables)
                if step_y:
                    out = (lane < 32) if step_y == 1 else (lane >= 96)
                    value = jnp.where(out, pltpu.roll(value, step_y % 8, 0), value)
                mate[FX_AT + 5 * end + i, pl.ds(pl.multiple_of(8 * p, 8), 8), :] = value

    def hand(v):
        return pltpu.make_async_copy(
            leaving.at[:, v + 1, pl.ds(8, 32), :], mate.at[pl.ds(19 * v, 19)], mate_sem.at[v]
        )

    def work(p, carry):
        for cp in load(p):
            cp.wait()
        faces(p)

        @pl.when(p == 0)
        def _():
            def after(v):
                @pl.when(v > 0)
                def _():
                    hand(v - 1).start()

            process(raw.at[0], leaving, stage, lanes_of, after)
            hand(7).start()

        return carry

    lax.fori_loop(0, 4, work, 0)
    for v in range(8):
        hand(v).wait()


def column_send(streamed, out, out_sem, leaver, p, v):
    return pltpu.make_async_copy(
        streamed.at[p - 1, :, v + 1, pl.ds(8, 32), :],
        out.at[block_at(p, leaver), :, :, pl.ds(pl.multiple_of(v * 128, 128), 128)],
        out_sem.at[p - 1, v],
    )


def early_kernel(migration, raw, after, out, streamed, stage, out_sem):
    del after
    lanes_of = lane_tables()
    leaver, _ = leaver_of(migration)
    send = functools.partial(column_send, streamed, out, out_sem, leaver)

    def block(p, carry):
        def after_column(v):
            @pl.when(v > 1)
            def _():
                send(p, v - 1).start()

        process(raw.at[p], streamed.at[p - 1], stage, lanes_of, after_column)
        return carry

    def finish(p, carry):
        for v in range(1, 7):
            send(p, v).wait()
        return carry

    end = early_blocks() + 1
    lax.fori_loop(1, end, block, 0)
    lax.fori_loop(1, end, finish, 0)


def late_kernel(neighbours, migration, raw, held, mine, got_in, after, out_in, out, streamed, got,
                stage, fx, rows, table, out_sem, got_sem, row_sem):
    del held, got_in, after, out_in
    lanes_of = lane_tables()
    leaver, moving = leaver_of(migration)
    sub = lax.broadcasted_iota(jnp.int32, (8, 128), 0)
    send = functools.partial(column_send, streamed, out, out_sem, leaver)
    for s, ref in enumerate((mine, got)):
        fx[s] = ref[pl.ds(FX_AT, 10)]

    @pl.when(jnp.logical_not(moving))
    def _():
        def keep(n, carry):
            got[n] = mine[n]
            return carry

        lax.fori_loop(0, FX_AT, keep, 0)

    for p in range(4):
        table[migration[block_at(p, leaver)] & 7] = p
        table[read(got, TAG_AT, 0, p) & 7] = 4 + p

    def incoming(b):
        found = {}
        for step_x, k in ((1, 1), (-1, 0)):
            code = table[neighbours[b, k] & 7]
            found[step_x] = (code >> 2, code & 3)
        return found

    def with_row(now, where, step_x, k, column):
        src, p = where
        home, start = (0, 0) if step_x == 1 else (7, 5)
        x = fx[src, start + k, pl.ds(pl.multiple_of(8 * p, 8), 8), :]
        return jnp.where(sub == home, pltpu.roll(x, (home - column) & 7, 0), now)

    def patch_column(xs, v, at):
        for step_x, comps in ((1, XP), (-1, XM)):
            for k, c in enumerate(comps):
                ref = at(c, 0 if step_x == 1 else 24)
                ref[...] = with_row(ref[...], xs[step_x], step_x, k, v)

    def streamed_at(p, v):
        return lambda c, row: streamed.at[p - 1, c, v + 1, pl.ds(8 + row, 8), :]

    xs = incoming(leaver)

    def arrived(v):
        return pltpu.make_async_copy(
            got.at[pl.ds(19 * v, 19)], out.at[leaver, :, :, pl.ds(128 * v, 128)], got_sem.at[v]
        )

    for v in range(8):
        patch_column(xs, v, lambda c, row: got.at[19 * v + c, pl.ds(row, 8), :])
        if 0 < v < 7:
            arrived(v).start()

    def send_rows(p):
        return [
            pltpu.make_async_copy(
                rows.at[p - 1, last, :, pl.ds(7 * last, 1), :],
                out.at[block_at(p, leaver), pl.ds(1, 14), pl.ds(31 * last, 1), pl.ds(128, 768)],
                row_sem.at[p - 1, last],
            )
            for last in range(2)
        ]

    def written(p, carry):
        xs = incoming(block_at(p, leaver))
        for last, step_x, comps in ((0, 1, XP), (1, -1, XM)):
            for c in range(1, 15):
                for v in range(1, 7):
                    now = streamed[p - 1, c, v + 1, pl.ds(8 + 24 * last, 8), :]
                    if c in comps:
                        now = with_row(now, xs[step_x], step_x, comps.index(c), v)
                    rows[p - 1, last, c - 1, :, pl.ds(128 * (v - 1), 128)] = now
        for cp in send_rows(p):
            cp.start()
        for v in (0, 7):
            patch_column(xs, v, streamed_at(p, v))
        return carry

    def remaining(p, carry):
        xs = incoming(block_at(p, leaver))

        def after_column(v):
            @pl.when(v > 0)
            def _():
                patch_column(xs, v - 1, streamed_at(p, v - 1))

            @pl.when(v > 1)
            def _():
                send(p, v - 1).start()

        process(raw.at[p], streamed.at[p - 1], stage, lanes_of, after_column)
        patch_column(xs, 7, streamed_at(p, 7))
        return carry

    def finish(p, carry):
        for v in range(1, 7):
            send(p, v).wait()
        return carry

    def finish_rows(p, carry):
        for cp in send_rows(p):
            cp.wait()
        return carry

    middle = early_blocks() + 1
    lax.fori_loop(1, middle, written, 0)
    lax.fori_loop(middle, 4, remaining, 0)
    lax.fori_loop(1, middle, finish_rows, 0)
    lax.fori_loop(middle, 4, finish, 0)
    for v in range(1, 7):
        arrived(v).wait()


def read(ref, at, row, segment):
    return ref[at, row, 32 * segment].astype(jnp.int32)


def select_kernel(mine, got, after, rise, fall, faces, table, places):
    del after
    lane = lax.broadcasted_iota(jnp.int32, (8, 128), 1)
    segment = lane >> 5
    for s, ref in enumerate((mine, got)):
        for high, at in enumerate((FU_AT, FD_AT)):
            faces[s, high] = ref[pl.ds(at, 5)]
        for p in range(4):
            table[read(ref, TAG_AT, 0, p) & 7] = 4 * s + p
    own = (device_index() & 1) * 4
    ups, downs = jnp.int32(0), jnp.int32(0)
    for s, ref in enumerate((mine, got)):
        for b in range(4):
            up = read(ref, TAG_AT, 1, b)
            slot = (own ^ (4 * s)) + b
            places[jnp.where(up == 1, ups, 4 + downs)] = slot
            ups, downs = ups + up, downs + 1 - up
    pair = (device_index() >> 1) << 3
    for high, halo in enumerate((rise, fall)):
        tag = jnp.zeros((8, 128), F32)
        where = []
        for m in range(4):
            slot = places[4 * high + m]
            code = table[slot]
            where.append((code >> 2, code & 3))
            tag = jnp.where(segment == m, jnp.full((8, 128), pair + slot, jnp.int32).astype(F32), tag)
        halo[20] = tag
        for i in range(5):
            for part in range(4):
                got_tile = None
                for m, (src, p) in enumerate(where):
                    x = pltpu.roll(faces[src, high, i, pl.ds(8 * part, 8), :], (32 * (4 + m - p)) & 127, 1)
                    got_tile = x if m == 0 else jnp.where(segment == m, x, got_tile)
                halo[4 * i + part] = got_tile


def last_kernel(neighbours, migration, mine, low, high, got, streamed_in, out_in,
                out, streamed, fu, fd, columns, table, got_sem, side_sem):
    del streamed_in, out_in
    pair = (device_index() >> 1) << 3
    leaver, _ = leaver_of(migration)
    lane = lax.broadcasted_iota(jnp.int32, (8, 128), 1)
    sub = lax.broadcasted_iota(jnp.int32, (8, 128), 0)

    for s, ref in enumerate((mine, got)):
        fu[s] = ref[pl.ds(FU_AT, 5)]
        fd[s] = ref[pl.ds(FD_AT, 5)]
    for n in range(20):
        fu[2, n // 4, pl.ds(8 * (n % 4), 8), :] = low[n]
        fd[2, n // 4, pl.ds(8 * (n % 4), 8), :] = high[n]
    for high_side in range(2):
        columns[high_side] = got[pl.ds(19 * 7 * high_side, 19)]

    for p in range(4):
        table[migration[block_at(p, leaver)] & 7] = p
        table[read(got, TAG_AT, 0, p) & 7] = 4 + p
        table[8 + (read(low, 20, 0, p) & 7)] = 8 + p
        table[16 + (read(high, 20, 0, p) & 7)] = 8 + p

    def find(b, k, beside):
        slot = neighbours[b, k]
        code = table[(slot & 7) + jnp.where((slot >> 3) << 3 == pair, 0, beside)]
        return code >> 2, code & 3

    def patch_columns(b, at):
        corners = {
            (1, 1): find(b, 5, 8), (-1, 1): find(b, 6, 8),
            (-1, -1): find(b, 4, 16), (1, -1): find(b, 7, 16),
        }
        for upper in (0, 1):
            comps, faces, home = (YD, fd, 3) if upper else (YU, fu, 0)
            source = find(b, 2 if upper else 3, 16 if upper else 8)
            edge = (lane >= 96) if upper else (lane < 32)

            def tile(where, i, part):
                src, p = where
                return pltpu.roll(faces[src, i, pl.ds(8 * part, 8), :], (32 * (home + 4 - p)) & 127, 1)

            for i, c in enumerate(comps):
                step_x, step_y, _ = VELOCITY[c]
                tiles = [tile(source, i, part) for part in range(4)]
                if step_x == 1:
                    near = [tile(corners[1, step_y], i, 3)] + tiles
                    near = [pltpu.roll(t, 1, 0) for t in near]
                    tiles = [jnp.where(sub == 0, near[q], near[q + 1]) for q in range(4)]
                elif step_x == -1:
                    near = tiles + [tile(corners[-1, step_y], i, 0)]
                    near = [pltpu.roll(t, 7, 0) for t in near]
                    tiles = [jnp.where(sub == 7, near[q + 1], near[q]) for q in range(4)]
                for part in range(4):
                    ref = at(c, part, upper)
                    ref[...] = jnp.where(edge, tiles[part], ref[...])

    def send_arrived(upper):
        return pltpu.make_async_copy(
            columns.at[upper], out.at[leaver, :, :, pl.ds(896 * upper, 128)], got_sem.at[upper]
        )

    patch_columns(leaver, lambda c, part, upper: columns.at[upper, c, pl.ds(8 * part, 8), :])
    for upper in range(2):
        send_arrived(upper).start()

    def send_sides(p):
        return [
            pltpu.make_async_copy(
                streamed.at[p - 1, :, 1 + 7 * upper, pl.ds(8, 32), :],
                out.at[block_at(p, leaver), :, :, pl.ds(896 * upper, 128)],
                side_sem.at[p - 1, upper],
            )
            for upper in range(2)
        ]

    def finish_block(p, carry):
        patch_columns(
            block_at(p, leaver),
            lambda c, part, upper: streamed.at[p - 1, c, 1 + 7 * upper, pl.ds(8 + 8 * part, 8), :],
        )
        for cp in send_sides(p):
            cp.start()
        return carry

    lax.fori_loop(1, 4, finish_block, 0)
    for p in range(1, 4):
        for cp in send_sides(p):
            cp.wait()
    for upper in range(2):
        send_arrived(upper).wait()


def route(shift, cross):
    count = lax.axis_size("gx") * lax.axis_size("gy")
    return [(d, ((d + shift) % count) ^ cross) for d in range(count)]


def on_device(populations, solid_share, migration, neighbours):
    populations = pltpu.with_memory_space_constraint(populations, pltpu.HBM)
    solid_share = pltpu.with_memory_space_constraint(solid_share, pltpu.HBM)
    migration = pltpu.with_memory_space_constraint(migration, pltpu.HBM)
    neighbours = pltpu.with_memory_space_constraint(neighbours, pltpu.HBM)
    dma = pltpu.SemaphoreType.DMA
    mib = 2**20
    stage = pltpu.VMEM((16, 32, 128), F32)
    stream_shape = pltpu.VMEM((3, 19, 10, 48, 128), F32)
    mate_shape = pltpu.VMEM((MATE, 32, 128), F32)
    halo_shape = pltpu.VMEM((HALO, 8, 128), F32)
    out_shape = jax.ShapeDtypeStruct((4, 19, 32, 1024), F32)

    def params(limit):
        return pltpu.CompilerParams(vmem_limit_bytes=limit * mib)

    def cost(flops, data):
        return pl.CostEstimate(flops=flops, bytes_accessed=data, transcendentals=0)

    slots_shape = pltpu.SMEM((4,), jnp.int32)
    near_shape = pltpu.SMEM((4, 8), jnp.int32)
    raw, mate, migration, neighbours = pl.pallas_call(
        first_kernel,
        name="faces_and_leaver",
        out_shape=(pltpu.VMEM((4, 20, 32, 1024), F32), mate_shape, slots_shape, near_shape),
        in_specs=[SMEM, SMEM, HBM, HBM],
        out_specs=(VMEM, VMEM, SMEM, SMEM),
        scratch_shapes=[pltpu.VMEM((19, 10, 48, 128), F32), stage, dma((4,)), dma((4,)), dma((8,))],
        compiler_params=params(8),
        cost_estimate=cost(20_000_000, 12_000_000),
    )(migration, neighbours, populations, solid_share)

    axes = ("gx", "gy")
    got = lax.ppermute(mate, axes, route(0, 1))

    out, streamed = pl.pallas_call(
        early_kernel,
        name="early_blocks",
        out_shape=(out_shape, stream_shape),
        in_specs=[SMEM, VMEM, VMEM],
        out_specs=(HBM, VMEM),
        scratch_shapes=[stage, dma((3, 8))],
        compiler_params=params(4),
        cost_estimate=cost(30_000_000, 16_000_000),
    )(migration, raw, mate)

    rise, fall = pl.pallas_call(
        select_kernel,
        name="select_faces",
        out_shape=(halo_shape, halo_shape),
        in_specs=[VMEM, VMEM, VMEM],
        out_specs=(VMEM, VMEM),
        scratch_shapes=[
            pltpu.VMEM((2, 2, 5, 32, 128), F32),
            pltpu.SMEM((8,), jnp.int32),
            pltpu.SMEM((8,), jnp.int32),
        ],
        compiler_params=params(4),
        cost_estimate=cost(1_000_000, 1_000_000),
    )(mate, got, streamed)
    high = lax.ppermute(fall, axes, route(-2, 0))
    low = lax.ppermute(rise, axes, route(2, 0))

    out, streamed, got = pl.pallas_call(
        late_kernel,
        name="late_blocks",
        out_shape=(out_shape, stream_shape, mate_shape),
        in_specs=[SMEM, SMEM] + [VMEM] * 5 + [HBM],
        out_specs=(HBM, VMEM, VMEM),
        input_output_aliases={7: 0, 3: 1, 5: 2},
        scratch_shapes=[
            stage,
            pltpu.VMEM((2, 10, 32, 128), F32),
            pltpu.VMEM((3, 2, 14, 8, 768), F32),
            pltpu.SMEM((8,), jnp.int32),
            dma((3, 8)), dma((8,)), dma((3, 2)),
        ],
        compiler_params=params(6),
        cost_estimate=cost(30_000_000, 16_000_000),
    )(neighbours, migration, raw, streamed, mate, got, fall, out)

    out, _ = pl.pallas_call(
        last_kernel,
        name="outer_columns",
        out_shape=(out_shape, stream_shape),
        in_specs=[SMEM, SMEM] + [VMEM] * 5 + [HBM],
        out_specs=(HBM, VMEM),
        input_output_aliases={7: 0, 6: 1},
        scratch_shapes=[
            pltpu.VMEM((3, 5, 32, 128), F32),
            pltpu.VMEM((3, 5, 32, 128), F32),
            pltpu.VMEM((2, 19, 32, 128), F32),
            pltpu.SMEM((24,), jnp.int32),
            dma((2,)), dma((3, 2)),
        ],
        compiler_params=params(6),
        cost_estimate=cost(1_000_000, 8_000_000),
    )(neighbours, migration, mate, low, high, got, streamed, out)
    return out


def solution(mesh):
    return jax.shard_map(
        on_device,
        mesh=mesh,
        in_specs=(
            P(("gx", "gy"), None, None, None),
            P(("gx", "gy"), None, None),
            P(("gx", "gy")),
            P(("gx", "gy"), None),
        ),
        out_specs=P(("gx", "gy"), None, None, None),
        check_vma=False,
    )
```

```python
import functools

import jax
import jax.numpy as jnp
from jax import lax
from jax.experimental import pallas as pl
from jax.experimental.pallas import tpu as pltpu
from jax.sharding import PartitionSpec as P

VELOCITY = [
    (0, 0, 0), (1, 0, 0), (-1, 0, 0), (0, 1, 0), (0, -1, 0), (0, 0, 1), (0, 0, -1),
    (1, 1, 0), (-1, -1, 0), (1, -1, 0), (-1, 1, 0), (1, 0, 1), (-1, 0, -1), (1, 0, -1),
    (-1, 0, 1), (0, 1, 1), (0, -1, -1), (0, 1, -1), (0, -1, 1),
]
XP = [1, 7, 9, 11, 13]
XM = [2, 8, 10, 12, 14]
YU = [3, 7, 10, 15, 17]
YD = [4, 8, 9, 16, 18]
F32 = jnp.float32
HBM = pl.BlockSpec(memory_space=pltpu.HBM)
VMEM = pl.BlockSpec(memory_space=pltpu.VMEM)
SMEM = pl.BlockSpec(memory_space=pltpu.SMEM)
FX_AT, FU_AT, FD_AT, TAG_AT, MATE = 152, 162, 167, 172, 173
HALO = 21


def collide(f, share):
    q = 1.0 - share
    s = [None] * 19
    d = [None] * 19
    for i in range(1, 19, 2):
        s[i] = f[i] + f[i + 1]
        d[i] = f[i] - f[i + 1]
    dxy, exy = s[7] + s[9], s[7] - s[9]
    dxz, exz = s[11] + s[13], s[11] - s[13]
    dyz, eyz = s[15] + s[17], s[15] - s[17]
    sx = (s[1] + s[3]) + s[5]
    sd = (dxy + dxz) + dyz
    rho = (f[0] + sx) + sd
    axy, bxy = d[7] + d[9], d[7] - d[9]
    axz, bxz = d[11] + d[13], d[11] - d[13]
    ayz, byz = d[15] + d[17], d[15] - d[17]
    tx, ty, tz = axy + axz, bxy + ayz, bxz + byz
    jx, jy, jz = d[1] + tx, d[3] + ty, d[5] + tz
    r = pl.reciprocal(rho, approx=True)
    r = r * (2.0 - rho * r)
    vx, vy, vz = jx * r, jy * r, jz * r
    ux, uy, uz = jx * vx, jy * vy, jz * vz
    j2 = (ux + uy) + uz
    iso_a = (-173.0 / 1800.0) * f[0] + (-4.0 / 45.0) * sx + ((-29.0 / 600.0) * sd + (197.0 / 1800.0) * j2)
    iso_d = (-23.0 / 900.0) * f[0] + (-1.0 / 36.0) * sx + ((-19.0 / 300.0) * sd + (-103.0 / 900.0) * j2)
    iso_0 = (53.0 / 60.0) * f[0] + (-7.0 / 15.0) * sx + ((-5.0 / 12.0) * sd + 0.65 * j2)

    def axis_even(x, dd, u):
        return q * ((11.0 / 15.0) * x + (-1.0 / 30.0) * dd + ((-23.0 / 60.0) * u + iso_a))

    def plane_even(x, dd, u):
        return q * ((-1.0 / 30.0) * x + (23.0 / 60.0) * dd + ((5.0 / 24.0) * u + iso_d))

    q4 = 0.4 * q
    q2 = 0.2 * q
    qm = 0.2475 * q
    ex, ey, ez = axis_even(s[1], dyz, ux), axis_even(s[3], dxz, uy), axis_even(s[5], dxy, uz)
    pyz, pxz, pxy = plane_even(s[1], dyz, ux), plane_even(s[3], dxz, uy), plane_even(s[5], dxy, uz)
    hxy, hxz, hyz = q4 * (exy - jx * vy), q4 * (exz - jx * vz), q4 * (eyz - jy * vz)
    hx = q2 * ((d[1] + d[1]) - tx)
    hy = q2 * ((d[3] + d[3]) - ty)
    hz = q2 * ((d[5] + d[5]) - tz)
    gx, gy, gz = 0.25 * hx, 0.25 * hy, 0.25 * hz
    mx, my, mz = qm * (axy - axz), qm * (ayz - bxy), qm * (bxz - byz)
    axy_o, bxy_o = mx - gx, -(my + gy)
    axz_o, bxz_o = -(mx + gx), mz - gz
    ayz_o, byz_o = my - gy, -(mz + gz)
    odd = {
        1: hx, 3: hy, 5: hz,
        7: axy_o + bxy_o, 9: axy_o - bxy_o,
        11: axz_o + bxz_o, 13: axz_o - bxz_o,
        15: ayz_o + byz_o, 17: ayz_o - byz_o,
    }
    even = {
        1: ex, 3: ey, 5: ez,
        7: pxy + hxy, 9: pxy - hxy,
        11: pxz + hxz, 13: pxz - hxz,
        15: pyz + hyz, 17: pyz - hyz,
    }
    post = [None] * 19
    post[0] = f[0] - q * iso_0
    for i in range(1, 19, 2):
        w = odd[i] + share * d[i]
        post[i] = (f[i] - even[i]) - w
        post[i + 1] = (f[i + 1] - even[i]) + w
    return post


def lane_tables():
    lane = lax.broadcasted_iota(jnp.int32, (8, 128), 1)
    tables = {}
    for step_y in (-1, 0, 1):
        for step_z in (-1, 1):
            tables[step_y, step_z] = ((lane - 32 * step_y) & 96) | ((lane - step_z) & 31)
    return lane, tables


def turn(x, step_y, step_z, tables):
    if step_z:
        return jnp.take_along_axis(x, tables[step_y, step_z], axis=1)
    return pltpu.roll(x, (32 * step_y) % 128, 1) if step_y else x


ORDER = [5, 11, 14, 6, 12, 13, 15, 17, 16, 18, 3, 7, 10, 4, 8, 9]


def collide_part(source, column, part, stage, result):
    at = pl.ds(pl.multiple_of(column * 128, 128), 128)
    rows = pl.ds(8 * part, 8)
    post = collide([source[c, rows, at] for c in range(19)], source[19, rows, at])
    for c in range(3):
        result[c, column + 1, pl.ds(8 + 8 * part + VELOCITY[c][0], 8), :] = post[c]
    for c in range(3, 19):
        stage[c - 3, rows, :] = post[c]


def turn_all(stage, column, result, lanes_of):
    lane, tables = lanes_of
    for c in ORDER:
        step_x, step_y, step_z = VELOCITY[c]
        out = (lane < 32) if step_y == 1 else (lane >= 96)
        for part in range(4):
            value = turn(stage[c - 3, pl.ds(8 * part, 8), :], step_y, step_z, tables)
            to = pl.ds(8 + 8 * part + step_x, 8)
            if step_y == 0:
                result[c, column + 1, to, :] = value
            else:
                pltpu.store(result.at[c, column + 1, to, :], value, mask=jnp.logical_not(out))
                pltpu.store(result.at[c, column + 1 + step_y, to, :], value, mask=out)


def process(source, result, stage, lanes_of, after, before=lambda i: None):
    def some(i, carry):
        before(i)
        for h in range(4):
            v = 4 * i + h
            for part in range(4):
                collide_part(source, v, part, stage, result)
            turn_all(stage, v, result, lanes_of)
            after(v)
        return carry

    lax.fori_loop(0, 2, some, 0)


def device_index():
    return lax.axis_index("gx") * lax.axis_size("gy") + lax.axis_index("gy")


def leaver_of(migration):
    base = device_index() * 4
    leaver = jnp.int32(0)
    moving = jnp.bool_(False)
    for b in (3, 2, 1, 0):
        away = migration[b] != base + b
        leaver = jnp.where(away, b, leaver)
        moving = jnp.logical_or(moving, away)
    return leaver, moving


def staying(j, leaver):
    return j + (j >= leaver).astype(jnp.int32)


def early_blocks():
    z = (device_index() >> 1) & 3
    return jnp.where(z == 0, 3, jnp.where(z == 3, 1, 2)).astype(jnp.int32)


def block_at(p, leaver):
    return jnp.where(p == 0, leaver, staying(p - 1, leaver))


def first_kernel(migration, neighbours, pop, share, raw, mate, slots, near, leaving, stage, half_sem, pop_sem, share_sem, mate_sem):
    lanes_of = lane_tables()
    lane, tables = lanes_of
    segment = lane >> 5
    sub = lax.broadcasted_iota(jnp.int32, (8, 128), 0)
    leaver, _ = leaver_of(migration)

    def load(p):
        b = block_at(p, leaver)
        return (
            pltpu.make_async_copy(pop.at[b], raw.at[p, pl.ds(0, 19)], pop_sem.at[p]),
            pltpu.make_async_copy(share.at[b], raw.at[p, 19], share_sem.at[p]),
        )

    def half(h):
        lanes = pl.ds(512 * h, 512)
        return (
            pltpu.make_async_copy(pop.at[leaver, :, :, lanes], raw.at[0, pl.ds(0, 19), :, lanes], half_sem.at[0, h]),
            pltpu.make_async_copy(share.at[leaver, :, lanes], raw.at[0, 19, :, lanes], half_sem.at[1, h]),
        )

    for cp in half(0) + half(1):
        cp.start()
    for p in range(1, 4):
        for cp in load(p):
            cp.start()
    for b in range(4):
        slots[b] = migration[b]
        for k in range(8):
            near[b, k] = neighbours[b, k]

    pair = (device_index() >> 1) << 3
    tag = jnp.zeros((8, 128), F32)
    for p in range(4):
        slot = migration[block_at(p, leaver)]
        above = (((neighbours[p, 2] >> 3) << 3) != pair).astype(jnp.int32)
        value = jnp.where(sub == 0, jnp.full((8, 128), slot, jnp.int32), jnp.full((8, 128), above, jnp.int32))
        tag = jnp.where(segment == p, value.astype(F32), tag)
    mate[TAG_AT, pl.ds(0, 8), :] = tag

    def faces(p):
        mine = segment == p
        for part in range(4):
            rows = pl.ds(8 * part, 8)

            def ends(c):
                return jnp.where(lane < 64, raw[p, c, rows, pl.ds(0, 128)], raw[p, c, rows, pl.ds(896, 128)])

            post = collide([ends(c) for c in range(19)], ends(19))
            for comps, at, shift in ((YU, FU_AT, 32 * p + 32), (YD, FD_AT, 32 * p)):
                for i, c in enumerate(comps):
                    value = turn(post[c], 0, VELOCITY[c][2], tables)
                    value = pltpu.roll(value, shift % 128, 1) if shift % 128 else value
                    pltpu.store(mate.at[at + i, rows, :], value, mask=mine)

        for end, comps in ((0, XP), (1, XM)):

            def packed(c):
                row = pl.ds(31 - 31 * end, 1)
                return jnp.concatenate([raw[p, c, row, pl.ds(128 * v, 128)] for v in range(8)], axis=0)

            post = collide([packed(c) for c in range(19)], packed(19))
            for i, c in enumerate(comps):
                _, step_y, step_z = VELOCITY[c]
                value = turn(post[c], step_y, step_z, tables)
                if step_y:
                    out = (lane < 32) if step_y == 1 else (lane >= 96)
                    value = jnp.where(out, pltpu.roll(value, step_y % 8, 0), value)
                mate[FX_AT + 5 * end + i, pl.ds(8 * p, 8), :] = value

    def hand(v):
        return pltpu.make_async_copy(
            leaving.at[:, v + 1, pl.ds(8, 32), :], mate.at[pl.ds(19 * v, 19)], mate_sem.at[v]
        )

    def before(i):
        for h in range(2):
            @pl.when(i == h)
            def _(h=h):
                for cp in half(h):
                    cp.wait()

    def after(v):
        @pl.when(v > 0)
        def _():
            hand(v - 1).start()

    process(raw.at[0], leaving, stage, lanes_of, after, before)
    hand(7).start()
    for group in ((0, 1), (2,), (3,)):
        for p in group:
            if p:
                for cp in load(p):
                    cp.wait()
        for p in group:
            faces(p)
    for v in range(8):
        hand(v).wait()


def column_send(streamed, out, out_sem, leaver, p, v):
    return pltpu.make_async_copy(
        streamed.at[p - 1, :, v + 1, pl.ds(8, 32), :],
        out.at[block_at(p, leaver), :, :, pl.ds(pl.multiple_of(v * 128, 128), 128)],
        out_sem.at[p - 1, v],
    )


def early_kernel(migration, raw, after, out, streamed, stage, out_sem):
    del after
    lanes_of = lane_tables()
    leaver, _ = leaver_of(migration)
    send = functools.partial(column_send, streamed, out, out_sem, leaver)

    def block(p, carry):
        def after_column(v):
            @pl.when(v > 1)
            def _():
                send(p, v - 1).start()

        process(raw.at[p], streamed.at[p - 1], stage, lanes_of, after_column)
        return carry

    def finish(p, carry):
        for v in range(1, 7):
            send(p, v).wait()
        return carry

    end = early_blocks() + 1
    lax.fori_loop(1, end, block, 0)
    lax.fori_loop(1, end, finish, 0)


def late_kernel(neighbours, migration, raw, held, mine, got_in, after, out_in, out, streamed, got,
                stage, fx, rows, table, out_sem, got_sem, row_sem):
    del held, got_in, after, out_in
    lanes_of = lane_tables()
    leaver, moving = leaver_of(migration)
    sub = lax.broadcasted_iota(jnp.int32, (8, 128), 0)
    send = functools.partial(column_send, streamed, out, out_sem, leaver)
    for s, ref in enumerate((mine, got)):
        fx[s] = ref[pl.ds(FX_AT, 10)]

    @pl.when(jnp.logical_not(moving))
    def _():
        def keep(n, carry):
            got[n] = mine[n]
            return carry

        lax.fori_loop(0, FX_AT, keep, 0)

    for p in range(4):
        table[migration[block_at(p, leaver)] & 7] = p
        table[read(got, TAG_AT, 0, p) & 7] = 4 + p

    def incoming(b):
        found = {}
        for step_x, k in ((1, 1), (-1, 0)):
            code = table[neighbours[b, k] & 7]
            found[step_x] = (code >> 2, code & 3)
        return found

    def with_row(now, where, step_x, k, column):
        src, p = where
        home, start = (0, 0) if step_x == 1 else (7, 5)
        x = fx[src, start + k, pl.ds(pl.multiple_of(8 * p, 8), 8), :]
        return jnp.where(sub == home, pltpu.roll(x, (home - column) & 7, 0), now)

    def patch_column(xs, v, at):
        for step_x, comps in ((1, XP), (-1, XM)):
            for k, c in enumerate(comps):
                ref = at(c, 0 if step_x == 1 else 24)
                ref[...] = with_row(ref[...], xs[step_x], step_x, k, v)

    def streamed_at(p, v):
        return lambda c, row: streamed.at[p - 1, c, v + 1, pl.ds(8 + row, 8), :]

    xs = incoming(leaver)

    def arrived(v):
        return pltpu.make_async_copy(
            got.at[pl.ds(19 * v, 19)], out.at[leaver, :, :, pl.ds(128 * v, 128)], got_sem.at[v]
        )

    for v in range(8):
        patch_column(xs, v, lambda c, row: got.at[19 * v + c, pl.ds(row, 8), :])
        if 0 < v < 7:
            arrived(v).start()

    def send_rows(p):
        return [
            pltpu.make_async_copy(
                rows.at[p - 1, last, :, pl.ds(7 * last, 1), :],
                out.at[block_at(p, leaver), pl.ds(1, 14), pl.ds(31 * last, 1), pl.ds(128, 768)],
                row_sem.at[p - 1, last],
            )
            for last in range(2)
        ]

    def written(p, carry):
        xs = incoming(block_at(p, leaver))
        for last, step_x, comps in ((0, 1, XP), (1, -1, XM)):
            for c in range(1, 15):
                for v in range(1, 7):
                    now = streamed[p - 1, c, v + 1, pl.ds(8 + 24 * last, 8), :]
                    if c in comps:
                        now = with_row(now, xs[step_x], step_x, comps.index(c), v)
                    rows[p - 1, last, c - 1, :, pl.ds(128 * (v - 1), 128)] = now
        for cp in send_rows(p):
            cp.start()
        for v in (0, 7):
            patch_column(xs, v, streamed_at(p, v))
        return carry

    def remaining(p, carry):
        xs = incoming(block_at(p, leaver))

        def after_column(v):
            @pl.when(v > 0)
            def _():
                patch_column(xs, v - 1, streamed_at(p, v - 1))

            @pl.when(v > 1)
            def _():
                send(p, v - 1).start()

        process(raw.at[p], streamed.at[p - 1], stage, lanes_of, after_column)
        patch_column(xs, 7, streamed_at(p, 7))
        return carry

    def finish(p, carry):
        for v in range(1, 7):
            send(p, v).wait()
        return carry

    def finish_rows(p, carry):
        for cp in send_rows(p):
            cp.wait()
        return carry

    middle = early_blocks() + 1
    lax.fori_loop(1, middle, written, 0)
    lax.fori_loop(middle, 4, remaining, 0)
    lax.fori_loop(1, middle, finish_rows, 0)
    lax.fori_loop(middle, 4, finish, 0)
    for v in range(1, 7):
        arrived(v).wait()


def read(ref, at, row, segment):
    return ref[at, row, 32 * segment].astype(jnp.int32)


def select_kernel(mine, got, after, rise, fall, faces, table, places):
    del after
    lane = lax.broadcasted_iota(jnp.int32, (8, 128), 1)
    segment = lane >> 5
    for s, ref in enumerate((mine, got)):
        for high, at in enumerate((FU_AT, FD_AT)):
            faces[s, high] = ref[pl.ds(at, 5)]
        for p in range(4):
            table[read(ref, TAG_AT, 0, p) & 7] = 4 * s + p
    own = (device_index() & 1) * 4
    ups, downs = jnp.int32(0), jnp.int32(0)
    for s, ref in enumerate((mine, got)):
        for b in range(4):
            up = read(ref, TAG_AT, 1, b)
            slot = (own ^ (4 * s)) + b
            places[jnp.where(up == 1, ups, 4 + downs)] = slot
            ups, downs = ups + up, downs + 1 - up
    pair = (device_index() >> 1) << 3
    for high, halo in enumerate((rise, fall)):
        tag = jnp.zeros((8, 128), F32)
        where = []
        for m in range(4):
            slot = places[4 * high + m]
            code = table[slot]
            where.append((code >> 2, code & 3))
            tag = jnp.where(segment == m, jnp.full((8, 128), pair + slot, jnp.int32).astype(F32), tag)
        halo[20] = tag
        for i in range(5):
            for part in range(4):
                got_tile = None
                for m, (src, p) in enumerate(where):
                    x = pltpu.roll(faces[src, high, i, pl.ds(8 * part, 8), :], (32 * (4 + m - p)) & 127, 1)
                    got_tile = x if m == 0 else jnp.where(segment == m, x, got_tile)
                halo[4 * i + part] = got_tile


def last_kernel(neighbours, migration, mine, low, high, got_in, streamed_in, out_in,
                out, streamed, got, fu, fd, table, got_sem, side_sem):
    del got_in, streamed_in, out_in
    pair = (device_index() >> 1) << 3
    leaver, _ = leaver_of(migration)
    lane = lax.broadcasted_iota(jnp.int32, (8, 128), 1)
    sub = lax.broadcasted_iota(jnp.int32, (8, 128), 0)

    for s, ref in enumerate((mine, got)):
        fu[s] = ref[pl.ds(FU_AT, 5)]
        fd[s] = ref[pl.ds(FD_AT, 5)]
    for n in range(20):
        fu[2, n // 4, pl.ds(8 * (n % 4), 8), :] = low[n]
        fd[2, n // 4, pl.ds(8 * (n % 4), 8), :] = high[n]

    for p in range(4):
        table[migration[block_at(p, leaver)] & 7] = p
        table[read(got, TAG_AT, 0, p) & 7] = 4 + p
        table[8 + (read(low, 20, 0, p) & 7)] = 8 + p
        table[16 + (read(high, 20, 0, p) & 7)] = 8 + p

    def find(b, k, beside):
        slot = neighbours[b, k]
        code = table[(slot & 7) + jnp.where((slot >> 3) << 3 == pair, 0, beside)]
        return code >> 2, code & 3

    def patch_columns(b, at):
        corners = {
            (1, 1): find(b, 5, 8), (-1, 1): find(b, 6, 8),
            (-1, -1): find(b, 4, 16), (1, -1): find(b, 7, 16),
        }
        for upper in (0, 1):
            comps, faces, home = (YD, fd, 3) if upper else (YU, fu, 0)
            source = find(b, 2 if upper else 3, 16 if upper else 8)
            edge = (lane >= 96) if upper else (lane < 32)

            def tile(where, i, part):
                src, p = where
                return pltpu.roll(faces[src, i, pl.ds(8 * part, 8), :], (32 * (home + 4 - p)) & 127, 1)

            for i, c in enumerate(comps):
                step_x, step_y, _ = VELOCITY[c]
                tiles = [tile(source, i, part) for part in range(4)]
                if step_x == 1:
                    near = [tile(corners[1, step_y], i, 3)] + tiles
                    near = [pltpu.roll(t, 1, 0) for t in near]
                    tiles = [jnp.where(sub == 0, near[q], near[q + 1]) for q in range(4)]
                elif step_x == -1:
                    near = tiles + [tile(corners[-1, step_y], i, 0)]
                    near = [pltpu.roll(t, 7, 0) for t in near]
                    tiles = [jnp.where(sub == 7, near[q + 1], near[q]) for q in range(4)]
                for part in range(4):
                    ref = at(c, part, upper)
                    ref[...] = jnp.where(edge, tiles[part], ref[...])

    def send_arrived(upper):
        return pltpu.make_async_copy(
            got.at[pl.ds(133 * upper, 19)], out.at[leaver, :, :, pl.ds(896 * upper, 128)], got_sem.at[upper]
        )

    patch_columns(leaver, lambda c, part, upper: got.at[133 * upper + c, pl.ds(8 * part, 8), :])
    for upper in range(2):
        send_arrived(upper).start()

    def send_sides(p):
        return [
            pltpu.make_async_copy(
                streamed.at[p - 1, :, 1 + 7 * upper, pl.ds(8, 32), :],
                out.at[block_at(p, leaver), :, :, pl.ds(896 * upper, 128)],
                side_sem.at[p - 1, upper],
            )
            for upper in range(2)
        ]

    def finish_block(p, carry):
        patch_columns(
            block_at(p, leaver),
            lambda c, part, upper: streamed.at[p - 1, c, 1 + 7 * upper, pl.ds(8 + 8 * part, 8), :],
        )
        for cp in send_sides(p):
            cp.start()
        return carry

    lax.fori_loop(1, 4, finish_block, 0)
    for p in range(1, 4):
        for cp in send_sides(p):
            cp.wait()
    for upper in range(2):
        send_arrived(upper).wait()


def route(shift, cross):
    count = lax.axis_size("gx") * lax.axis_size("gy")
    return [(d, ((d + shift) % count) ^ cross) for d in range(count)]


def on_device(populations, solid_share, migration, neighbours):
    populations = pltpu.with_memory_space_constraint(populations, pltpu.HBM)
    solid_share = pltpu.with_memory_space_constraint(solid_share, pltpu.HBM)
    migration = pltpu.with_memory_space_constraint(migration, pltpu.HBM)
    neighbours = pltpu.with_memory_space_constraint(neighbours, pltpu.HBM)
    dma = pltpu.SemaphoreType.DMA
    mib = 2**20
    stage = pltpu.VMEM((16, 32, 128), F32)
    stream_shape = pltpu.VMEM((3, 19, 10, 48, 128), F32)
    mate_shape = pltpu.VMEM((MATE, 32, 128), F32)
    halo_shape = pltpu.VMEM((HALO, 8, 128), F32)
    out_shape = jax.ShapeDtypeStruct((4, 19, 32, 1024), F32)

    def params(limit):
        return pltpu.CompilerParams(vmem_limit_bytes=limit * mib)

    def cost(flops, data):
        return pl.CostEstimate(flops=flops, bytes_accessed=data, transcendentals=0)

    slots_shape = pltpu.SMEM((4,), jnp.int32)
    near_shape = pltpu.SMEM((4, 8), jnp.int32)
    raw, mate, migration, neighbours = pl.pallas_call(
        first_kernel,
        name="faces_and_leaver",
        out_shape=(pltpu.VMEM((4, 20, 32, 1024), F32), mate_shape, slots_shape, near_shape),
        in_specs=[SMEM, SMEM, HBM, HBM],
        out_specs=(VMEM, VMEM, SMEM, SMEM),
        scratch_shapes=[pltpu.VMEM((19, 10, 48, 128), F32), stage, dma((2, 2)), dma((4,)), dma((4,)), dma((8,))],
        compiler_params=params(8),
        cost_estimate=cost(20_000_000, 12_000_000),
    )(migration, neighbours, populations, solid_share)

    axes = ("gx", "gy")
    got = lax.ppermute(mate, axes, route(0, 1))

    out, streamed = pl.pallas_call(
        early_kernel,
        name="early_blocks",
        out_shape=(out_shape, stream_shape),
        in_specs=[SMEM, VMEM, VMEM],
        out_specs=(HBM, VMEM),
        scratch_shapes=[stage, dma((3, 8))],
        compiler_params=params(4),
        cost_estimate=cost(30_000_000, 16_000_000),
    )(migration, raw, mate)

    rise, fall = pl.pallas_call(
        select_kernel,
        name="select_faces",
        out_shape=(halo_shape, halo_shape),
        in_specs=[VMEM, VMEM, VMEM],
        out_specs=(VMEM, VMEM),
        scratch_shapes=[
            pltpu.VMEM((2, 2, 5, 32, 128), F32),
            pltpu.SMEM((8,), jnp.int32),
            pltpu.SMEM((8,), jnp.int32),
        ],
        compiler_params=params(4),
        cost_estimate=cost(1_000_000, 1_000_000),
    )(mate, got, streamed)
    high = lax.ppermute(fall, axes, route(-2, 0))
    low = lax.ppermute(rise, axes, route(2, 0))

    out, streamed, got = pl.pallas_call(
        late_kernel,
        name="late_blocks",
        out_shape=(out_shape, stream_shape, mate_shape),
        in_specs=[SMEM, SMEM] + [VMEM] * 5 + [HBM],
        out_specs=(HBM, VMEM, VMEM),
        input_output_aliases={7: 0, 3: 1, 5: 2},
        scratch_shapes=[
            stage,
            pltpu.VMEM((2, 10, 32, 128), F32),
            pltpu.VMEM((3, 2, 14, 8, 768), F32),
            pltpu.SMEM((8,), jnp.int32),
            dma((3, 8)), dma((8,)), dma((3, 2)),
        ],
        compiler_params=params(6),
        cost_estimate=cost(30_000_000, 16_000_000),
    )(neighbours, migration, raw, streamed, mate, got, fall, out)

    out, _, _ = pl.pallas_call(
        last_kernel,
        name="outer_columns",
        out_shape=(out_shape, stream_shape, mate_shape),
        in_specs=[SMEM, SMEM] + [VMEM] * 5 + [HBM],
        out_specs=(HBM, VMEM, VMEM),
        input_output_aliases={7: 0, 6: 1, 5: 2},
        scratch_shapes=[
            pltpu.VMEM((3, 5, 32, 128), F32),
            pltpu.VMEM((3, 5, 32, 128), F32),
            pltpu.SMEM((24,), jnp.int32),
            dma((2,)), dma((3, 2)),
        ],
        compiler_params=params(6),
        cost_estimate=cost(1_000_000, 8_000_000),
    )(neighbours, migration, mate, low, high, got, streamed, out)
    return out


def solution(mesh):
    return jax.shard_map(
        on_device,
        mesh=mesh,
        in_specs=(
            P(("gx", "gy"), None, None, None),
            P(("gx", "gy"), None, None),
            P(("gx", "gy")),
            P(("gx", "gy"), None),
        ),
        out_specs=P(("gx", "gy"), None, None, None),
        check_vma=False,
    )
```

```python
import functools

import jax
import jax.numpy as jnp
from jax import lax
from jax.experimental import pallas as pl
from jax.experimental.pallas import tpu as pltpu
from jax.sharding import PartitionSpec as P

VELOCITY = [
    (0, 0, 0), (1, 0, 0), (-1, 0, 0), (0, 1, 0), (0, -1, 0), (0, 0, 1), (0, 0, -1),
    (1, 1, 0), (-1, -1, 0), (1, -1, 0), (-1, 1, 0), (1, 0, 1), (-1, 0, -1), (1, 0, -1),
    (-1, 0, 1), (0, 1, 1), (0, -1, -1), (0, 1, -1), (0, -1, 1),
]
XP = [1, 7, 9, 11, 13]
XM = [2, 8, 10, 12, 14]
YU = [3, 7, 10, 15, 17]
YD = [4, 8, 9, 16, 18]
F32 = jnp.float32
HBM = pl.BlockSpec(memory_space=pltpu.HBM)
VMEM = pl.BlockSpec(memory_space=pltpu.VMEM)
SMEM = pl.BlockSpec(memory_space=pltpu.SMEM)
FX_AT, FU_AT, FD_AT, TAG_AT, MATE = 152, 162, 167, 172, 173
HALO = 21


def collide(f, share):
    q = 1.0 - share
    s = [None] * 19
    d = [None] * 19
    for i in range(1, 19, 2):
        s[i] = f[i] + f[i + 1]
        d[i] = f[i] - f[i + 1]
    dxy, exy = s[7] + s[9], s[7] - s[9]
    dxz, exz = s[11] + s[13], s[11] - s[13]
    dyz, eyz = s[15] + s[17], s[15] - s[17]
    sx = (s[1] + s[3]) + s[5]
    sd = (dxy + dxz) + dyz
    rho = (f[0] + sx) + sd
    axy, bxy = d[7] + d[9], d[7] - d[9]
    axz, bxz = d[11] + d[13], d[11] - d[13]
    ayz, byz = d[15] + d[17], d[15] - d[17]
    tx, ty, tz = axy + axz, bxy + ayz, bxz + byz
    jx, jy, jz = d[1] + tx, d[3] + ty, d[5] + tz
    r = pl.reciprocal(rho, approx=True)
    r = r * (2.0 - rho * r)
    vx, vy, vz = jx * r, jy * r, jz * r
    ux, uy, uz = jx * vx, jy * vy, jz * vz
    j2 = (ux + uy) + uz
    iso_a = (-173.0 / 1800.0) * f[0] + (-4.0 / 45.0) * sx + ((-29.0 / 600.0) * sd + (197.0 / 1800.0) * j2)
    iso_d = (-23.0 / 900.0) * f[0] + (-1.0 / 36.0) * sx + ((-19.0 / 300.0) * sd + (-103.0 / 900.0) * j2)
    iso_0 = (53.0 / 60.0) * f[0] + (-7.0 / 15.0) * sx + ((-5.0 / 12.0) * sd + 0.65 * j2)

    def axis_even(x, dd, u):
        return q * ((11.0 / 15.0) * x + (-1.0 / 30.0) * dd + ((-23.0 / 60.0) * u + iso_a))

    def plane_even(x, dd, u):
        return q * ((-1.0 / 30.0) * x + (23.0 / 60.0) * dd + ((5.0 / 24.0) * u + iso_d))

    q4 = 0.4 * q
    q2 = 0.2 * q
    qm = 0.2475 * q
    ex, ey, ez = axis_even(s[1], dyz, ux), axis_even(s[3], dxz, uy), axis_even(s[5], dxy, uz)
    pyz, pxz, pxy = plane_even(s[1], dyz, ux), plane_even(s[3], dxz, uy), plane_even(s[5], dxy, uz)
    hxy, hxz, hyz = q4 * (exy - jx * vy), q4 * (exz - jx * vz), q4 * (eyz - jy * vz)
    hx = q2 * ((d[1] + d[1]) - tx)
    hy = q2 * ((d[3] + d[3]) - ty)
    hz = q2 * ((d[5] + d[5]) - tz)
    gx, gy, gz = 0.25 * hx, 0.25 * hy, 0.25 * hz
    mx, my, mz = qm * (axy - axz), qm * (ayz - bxy), qm * (bxz - byz)
    axy_o, bxy_o = mx - gx, -(my + gy)
    axz_o, bxz_o = -(mx + gx), mz - gz
    ayz_o, byz_o = my - gy, -(mz + gz)
    odd = {
        1: hx, 3: hy, 5: hz,
        7: axy_o + bxy_o, 9: axy_o - bxy_o,
        11: axz_o + bxz_o, 13: axz_o - bxz_o,
        15: ayz_o + byz_o, 17: ayz_o - byz_o,
    }
    even = {
        1: ex, 3: ey, 5: ez,
        7: pxy + hxy, 9: pxy - hxy,
        11: pxz + hxz, 13: pxz - hxz,
        15: pyz + hyz, 17: pyz - hyz,
    }
    post = [None] * 19
    post[0] = f[0] - q * iso_0
    for i in range(1, 19, 2):
        w = odd[i] + share * d[i]
        post[i] = (f[i] - even[i]) - w
        post[i + 1] = (f[i + 1] - even[i]) + w
    return post


def lane_tables():
    lane = lax.broadcasted_iota(jnp.int32, (8, 128), 1)
    tables = {}
    for step_y in (-1, 0, 1):
        for step_z in (-1, 1):
            tables[step_y, step_z] = ((lane - 32 * step_y) & 96) | ((lane - step_z) & 31)
    return lane, tables


def turn(x, step_y, step_z, tables):
    if step_z:
        return jnp.take_along_axis(x, tables[step_y, step_z], axis=1)
    return pltpu.roll(x, (32 * step_y) % 128, 1) if step_y else x


ORDER = [5, 11, 14, 6, 12, 13, 15, 17, 16, 18, 3, 7, 10, 4, 8, 9]


def collide_part(source, column, part, stage, result):
    at = pl.ds(pl.multiple_of(column * 128, 128), 128)
    rows = pl.ds(8 * part, 8)
    post = collide([source[c, rows, at] for c in range(19)], source[19, rows, at])
    for c in range(3):
        result[c, column + 1, pl.ds(8 + 8 * part + VELOCITY[c][0], 8), :] = post[c]
    for c in range(3, 19):
        stage[c - 3, rows, :] = post[c]


def turn_all(stage, column, result, lanes_of):
    lane, tables = lanes_of
    for c in ORDER:
        step_x, step_y, step_z = VELOCITY[c]
        out = (lane < 32) if step_y == 1 else (lane >= 96)
        for part in range(4):
            value = turn(stage[c - 3, pl.ds(8 * part, 8), :], step_y, step_z, tables)
            to = pl.ds(8 + 8 * part + step_x, 8)
            if step_y == 0:
                result[c, column + 1, to, :] = value
            else:
                pltpu.store(result.at[c, column + 1, to, :], value, mask=jnp.logical_not(out))
                pltpu.store(result.at[c, column + 1 + step_y, to, :], value, mask=out)


def process(source, result, stage, lanes_of, after, before=lambda i: None):
    def some(i, carry):
        before(i)
        for h in range(4):
            v = 4 * i + h
            for part in range(4):
                collide_part(source, v, part, stage, result)
            turn_all(stage, v, result, lanes_of)
            after(v)
        return carry

    lax.fori_loop(0, 2, some, 0)


def device_index():
    return lax.axis_index("gx") * lax.axis_size("gy") + lax.axis_index("gy")


def leaver_of(migration):
    base = device_index() * 4
    leaver = jnp.int32(0)
    moving = jnp.bool_(False)
    for b in (3, 2, 1, 0):
        away = migration[b] != base + b
        leaver = jnp.where(away, b, leaver)
        moving = jnp.logical_or(moving, away)
    return leaver, moving


def staying(j, leaver):
    return j + (j >= leaver).astype(jnp.int32)


def early_blocks():
    z = (device_index() >> 1) & 3
    return jnp.where(z == 0, 3, jnp.where(z == 3, 1, 2)).astype(jnp.int32)


def block_at(p, leaver):
    return jnp.where(p == 0, leaver, staying(p - 1, leaver))


def first_kernel(migration, neighbours, pop, share, raw, mate, slots, near, leaving, stage, half_sem, pop_sem, share_sem, mate_sem):
    lanes_of = lane_tables()
    lane, tables = lanes_of
    segment = lane >> 5
    sub = lax.broadcasted_iota(jnp.int32, (8, 128), 0)
    leaver, _ = leaver_of(migration)

    def load(p):
        b = block_at(p, leaver)
        return (
            pltpu.make_async_copy(pop.at[b], raw.at[p, pl.ds(0, 19)], pop_sem.at[p]),
            pltpu.make_async_copy(share.at[b], raw.at[p, 19], share_sem.at[p]),
        )

    def half(h):
        lanes = pl.ds(512 * h, 512)
        return (
            pltpu.make_async_copy(pop.at[leaver, :, :, lanes], raw.at[0, pl.ds(0, 19), :, lanes], half_sem.at[0, h]),
            pltpu.make_async_copy(share.at[leaver, :, lanes], raw.at[0, 19, :, lanes], half_sem.at[1, h]),
        )

    for cp in half(0) + half(1):
        cp.start()
    for p in range(1, 4):
        for cp in load(p):
            cp.start()
    for b in range(4):
        slots[b] = migration[b]
        for k in range(8):
            near[b, k] = neighbours[b, k]

    pair = (device_index() >> 1) << 3
    tag = jnp.zeros((8, 128), F32)
    for p in range(4):
        slot = migration[block_at(p, leaver)]
        above = (((neighbours[p, 2] >> 3) << 3) != pair).astype(jnp.int32)
        value = jnp.where(sub == 0, jnp.full((8, 128), slot, jnp.int32), jnp.full((8, 128), above, jnp.int32))
        tag = jnp.where(segment == p, value.astype(F32), tag)
    mate[TAG_AT, pl.ds(0, 8), :] = tag

    def faces(p):
        mine = segment == p
        for part in range(4):
            rows = pl.ds(8 * part, 8)

            def ends(c):
                return jnp.where(lane < 64, raw[p, c, rows, pl.ds(0, 128)], raw[p, c, rows, pl.ds(896, 128)])

            post = collide([ends(c) for c in range(19)], ends(19))
            for comps, at, shift in ((YU, FU_AT, 32 * p + 32), (YD, FD_AT, 32 * p)):
                for i, c in enumerate(comps):
                    value = turn(post[c], 0, VELOCITY[c][2], tables)
                    value = pltpu.roll(value, shift % 128, 1) if shift % 128 else value
                    pltpu.store(mate.at[at + i, rows, :], value, mask=mine)

        for end, comps in ((0, XP), (1, XM)):

            def packed(c):
                row = pl.ds(31 - 31 * end, 1)
                return jnp.concatenate([raw[p, c, row, pl.ds(128 * v, 128)] for v in range(8)], axis=0)

            post = collide([packed(c) for c in range(19)], packed(19))
            for i, c in enumerate(comps):
                _, step_y, step_z = VELOCITY[c]
                value = turn(post[c], step_y, step_z, tables)
                if step_y:
                    out = (lane < 32) if step_y == 1 else (lane >= 96)
                    value = jnp.where(out, pltpu.roll(value, step_y % 8, 0), value)
                mate[FX_AT + 5 * end + i, pl.ds(8 * p, 8), :] = value

    def hand(v):
        return pltpu.make_async_copy(
            leaving.at[:, v + 1, pl.ds(8, 32), :], mate.at[pl.ds(19 * v, 19)], mate_sem.at[v]
        )

    def before(i):
        for h in range(2):
            @pl.when(i == h)
            def _(h=h):
                for cp in half(h):
                    cp.wait()

    def after(v):
        @pl.when(v > 0)
        def _():
            hand(v - 1).start()

    process(raw.at[0], leaving, stage, lanes_of, after, before)
    hand(7).start()
    for group in ((0, 1), (2,), (3,)):
        for p in group:
            if p:
                for cp in load(p):
                    cp.wait()
        for p in group:
            faces(p)
    for v in range(8):
        hand(v).wait()


def column_send(streamed, out, out_sem, leaver, p, v):
    return pltpu.make_async_copy(
        streamed.at[p - 1, :, v + 1, pl.ds(8, 32), :],
        out.at[block_at(p, leaver), :, :, pl.ds(pl.multiple_of(v * 128, 128), 128)],
        out_sem.at[p - 1, v],
    )


def early_kernel(migration, raw, after, out, streamed, stage, out_sem):
    del after
    lanes_of = lane_tables()
    leaver, _ = leaver_of(migration)
    send = functools.partial(column_send, streamed, out, out_sem, leaver)

    def block(p, carry):
        def after_column(v):
            @pl.when(v > 1)
            def _():
                send(p, v - 1).start()

        process(raw.at[p], streamed.at[p - 1], stage, lanes_of, after_column)
        return carry

    def finish(p, carry):
        for v in range(1, 7):
            send(p, v).wait()
        return carry

    end = early_blocks() + 1
    lax.fori_loop(1, end, block, 0)
    lax.fori_loop(1, end, finish, 0)


def late_kernel(neighbours, migration, raw, held, mine, got_in, after, out_in, out, streamed, got,
                stage, fx, rows, table, out_sem, got_sem, row_sem, still_sem):
    del held, got_in, after, out_in
    lanes_of = lane_tables()
    leaver, moving = leaver_of(migration)
    sub = lax.broadcasted_iota(jnp.int32, (8, 128), 0)
    send = functools.partial(column_send, streamed, out, out_sem, leaver)
    for s, ref in enumerate((mine, got)):
        fx[s] = ref[pl.ds(FX_AT, 10)]

    @pl.when(jnp.logical_not(moving))
    def _():
        def keep(n, carry):
            got[n] = mine[n]
            return carry

        lax.fori_loop(0, FX_AT, keep, 0)

    for p in range(4):
        table[migration[block_at(p, leaver)] & 7] = p
        table[read(got, TAG_AT, 0, p) & 7] = 4 + p

    def incoming(b):
        found = {}
        for step_x, k in ((1, 1), (-1, 0)):
            code = table[neighbours[b, k] & 7]
            found[step_x] = (code >> 2, code & 3)
        return found

    def with_row(now, where, step_x, k, column):
        src, p = where
        home, start = (0, 0) if step_x == 1 else (7, 5)
        x = fx[src, start + k, pl.ds(pl.multiple_of(8 * p, 8), 8), :]
        return jnp.where(sub == home, pltpu.roll(x, (home - column) & 7, 0), now)

    def patch_column(xs, v, at):
        for step_x, comps in ((1, XP), (-1, XM)):
            for k, c in enumerate(comps):
                ref = at(c, 0 if step_x == 1 else 24)
                ref[...] = with_row(ref[...], xs[step_x], step_x, k, v)

    def streamed_at(p, v):
        return lambda c, row: streamed.at[p - 1, c, v + 1, pl.ds(8 + row, 8), :]

    xs = incoming(leaver)

    def arrived(v):
        return pltpu.make_async_copy(
            got.at[pl.ds(19 * v, 19)], out.at[leaver, :, :, pl.ds(128 * v, 128)], got_sem.at[v]
        )

    def still(p, upper):
        few, at = pl.ds(0, 3), pl.ds(896 * upper, 128)
        source = got.at[pl.ds(133 * upper, 3)] if p is None else streamed.at[p - 1, few, 1 + 7 * upper, pl.ds(8, 32), :]
        b = leaver if p is None else block_at(p, leaver)
        return pltpu.make_async_copy(source, out.at[b, few, :, at], still_sem.at[0 if p is None else p, upper])

    for v in range(8):
        patch_column(xs, v, lambda c, row: got.at[19 * v + c, pl.ds(row, 8), :])
        if 0 < v < 7:
            arrived(v).start()
        else:
            still(None, v // 7).start()

    def send_rows(p):
        return [
            pltpu.make_async_copy(
                rows.at[p - 1, last, :, pl.ds(7 * last, 1), :],
                out.at[block_at(p, leaver), pl.ds(1, 14), pl.ds(31 * last, 1), pl.ds(128, 768)],
                row_sem.at[p - 1, last],
            )
            for last in range(2)
        ]

    def written(p, carry):
        xs = incoming(block_at(p, leaver))
        for last, step_x, comps in ((0, 1, XP), (1, -1, XM)):
            for c in range(1, 15):
                for v in range(1, 7):
                    now = streamed[p - 1, c, v + 1, pl.ds(8 + 24 * last, 8), :]
                    if c in comps:
                        now = with_row(now, xs[step_x], step_x, comps.index(c), v)
                    rows[p - 1, last, c - 1, :, pl.ds(128 * (v - 1), 128)] = now
        for cp in send_rows(p):
            cp.start()
        for v in (0, 7):
            patch_column(xs, v, streamed_at(p, v))
            still(p, v // 7).start()
        return carry

    def remaining(p, carry):
        xs = incoming(block_at(p, leaver))

        def after_column(v):
            @pl.when(v > 0)
            def _():
                patch_column(xs, v - 1, streamed_at(p, v - 1))

            @pl.when(v > 1)
            def _():
                send(p, v - 1).start()

        process(raw.at[p], streamed.at[p - 1], stage, lanes_of, after_column)
        patch_column(xs, 7, streamed_at(p, 7))
        for upper in range(2):
            still(p, upper).start()
        return carry

    def finish(p, carry):
        for v in range(1, 7):
            send(p, v).wait()
        return carry

    def finish_rows(p, carry):
        for cp in send_rows(p):
            cp.wait()
        return carry

    middle = early_blocks() + 1
    lax.fori_loop(1, middle, written, 0)
    lax.fori_loop(middle, 4, remaining, 0)
    lax.fori_loop(1, middle, finish_rows, 0)
    lax.fori_loop(middle, 4, finish, 0)
    for v in range(1, 7):
        arrived(v).wait()
    for upper in range(2):
        still(None, upper).wait()
        for p in range(1, 4):
            still(p, upper).wait()


def read(ref, at, row, segment):
    return ref[at, row, 32 * segment].astype(jnp.int32)


def select_kernel(mine, got, after, rise, fall, faces, table, places):
    del after
    lane = lax.broadcasted_iota(jnp.int32, (8, 128), 1)
    segment = lane >> 5
    for s, ref in enumerate((mine, got)):
        for high, at in enumerate((FU_AT, FD_AT)):
            faces[s, high] = ref[pl.ds(at, 5)]
        for p in range(4):
            table[read(ref, TAG_AT, 0, p) & 7] = 4 * s + p
    own = (device_index() & 1) * 4
    ups, downs = jnp.int32(0), jnp.int32(0)
    for s, ref in enumerate((mine, got)):
        for b in range(4):
            up = read(ref, TAG_AT, 1, b)
            slot = (own ^ (4 * s)) + b
            places[jnp.where(up == 1, ups, 4 + downs)] = slot
            ups, downs = ups + up, downs + 1 - up
    pair = (device_index() >> 1) << 3
    for high, halo in enumerate((rise, fall)):
        tag = jnp.zeros((8, 128), F32)
        where = []
        for m in range(4):
            slot = places[4 * high + m]
            code = table[slot]
            where.append((code >> 2, code & 3))
            tag = jnp.where(segment == m, jnp.full((8, 128), pair + slot, jnp.int32).astype(F32), tag)
        halo[20] = tag
        for i in range(5):
            for part in range(4):
                got_tile = None
                for m, (src, p) in enumerate(where):
                    x = pltpu.roll(faces[src, high, i, pl.ds(8 * part, 8), :], (32 * (4 + m - p)) & 127, 1)
                    got_tile = x if m == 0 else jnp.where(segment == m, x, got_tile)
                halo[4 * i + part] = got_tile


def last_kernel(neighbours, migration, mine, low, high, got_in, streamed_in, out_in,
                out, streamed, got, fu, fd, table, got_sem, side_sem):
    del got_in, streamed_in, out_in
    pair = (device_index() >> 1) << 3
    leaver, _ = leaver_of(migration)
    lane = lax.broadcasted_iota(jnp.int32, (8, 128), 1)
    sub = lax.broadcasted_iota(jnp.int32, (8, 128), 0)

    for s, ref in enumerate((mine, got)):
        fu[s] = ref[pl.ds(FU_AT, 5)]
        fd[s] = ref[pl.ds(FD_AT, 5)]
    for n in range(20):
        fu[2, n // 4, pl.ds(8 * (n % 4), 8), :] = low[n]
        fd[2, n // 4, pl.ds(8 * (n % 4), 8), :] = high[n]

    for p in range(4):
        table[migration[block_at(p, leaver)] & 7] = p
        table[read(got, TAG_AT, 0, p) & 7] = 4 + p
        table[8 + (read(low, 20, 0, p) & 7)] = 8 + p
        table[16 + (read(high, 20, 0, p) & 7)] = 8 + p

    def find(b, k, beside):
        slot = neighbours[b, k]
        code = table[(slot & 7) + jnp.where((slot >> 3) << 3 == pair, 0, beside)]
        return code >> 2, code & 3

    def patch_columns(b, at):
        corners = {
            (1, 1): find(b, 5, 8), (-1, 1): find(b, 6, 8),
            (-1, -1): find(b, 4, 16), (1, -1): find(b, 7, 16),
        }
        for upper in (0, 1):
            comps, faces, home = (YD, fd, 3) if upper else (YU, fu, 0)
            source = find(b, 2 if upper else 3, 16 if upper else 8)
            edge = (lane >= 96) if upper else (lane < 32)

            def tile(where, i, part):
                src, p = where
                return pltpu.roll(faces[src, i, pl.ds(8 * part, 8), :], (32 * (home + 4 - p)) & 127, 1)

            for i, c in enumerate(comps):
                step_x, step_y, _ = VELOCITY[c]
                tiles = [tile(source, i, part) for part in range(4)]
                if step_x == 1:
                    near = [tile(corners[1, step_y], i, 3)] + tiles
                    near = [pltpu.roll(t, 1, 0) for t in near]
                    tiles = [jnp.where(sub == 0, near[q], near[q + 1]) for q in range(4)]
                elif step_x == -1:
                    near = tiles + [tile(corners[-1, step_y], i, 0)]
                    near = [pltpu.roll(t, 7, 0) for t in near]
                    tiles = [jnp.where(sub == 7, near[q + 1], near[q]) for q in range(4)]
                for part in range(4):
                    ref = at(c, part, upper)
                    ref[...] = jnp.where(edge, tiles[part], ref[...])

    def send_arrived(upper):
        return pltpu.make_async_copy(
            got.at[pl.ds(133 * upper + 3, 16)],
            out.at[leaver, pl.ds(3, 16), :, pl.ds(896 * upper, 128)],
            got_sem.at[upper],
        )

    patch_columns(leaver, lambda c, part, upper: got.at[133 * upper + c, pl.ds(8 * part, 8), :])
    for upper in range(2):
        send_arrived(upper).start()

    def send_sides(p):
        return [
            pltpu.make_async_copy(
                streamed.at[p - 1, pl.ds(3, 16), 1 + 7 * upper, pl.ds(8, 32), :],
                out.at[block_at(p, leaver), pl.ds(3, 16), :, pl.ds(896 * upper, 128)],
                side_sem.at[p - 1, upper],
            )
            for upper in range(2)
        ]

    def finish_block(p, carry):
        patch_columns(
            block_at(p, leaver),
            lambda c, part, upper: streamed.at[p - 1, c, 1 + 7 * upper, pl.ds(8 + 8 * part, 8), :],
        )
        for cp in send_sides(p):
            cp.start()
        return carry

    lax.fori_loop(1, 4, finish_block, 0)
    for p in range(1, 4):
        for cp in send_sides(p):
            cp.wait()
    for upper in range(2):
        send_arrived(upper).wait()


def route(shift, cross):
    count = lax.axis_size("gx") * lax.axis_size("gy")
    return [(d, ((d + shift) % count) ^ cross) for d in range(count)]


def on_device(populations, solid_share, migration, neighbours):
    populations = pltpu.with_memory_space_constraint(populations, pltpu.HBM)
    solid_share = pltpu.with_memory_space_constraint(solid_share, pltpu.HBM)
    migration = pltpu.with_memory_space_constraint(migration, pltpu.HBM)
    neighbours = pltpu.with_memory_space_constraint(neighbours, pltpu.HBM)
    dma = pltpu.SemaphoreType.DMA
    mib = 2**20
    stage = pltpu.VMEM((16, 32, 128), F32)
    stream_shape = pltpu.VMEM((3, 19, 10, 48, 128), F32)
    mate_shape = pltpu.VMEM((MATE, 32, 128), F32)
    halo_shape = pltpu.VMEM((HALO, 8, 128), F32)
    out_shape = jax.ShapeDtypeStruct((4, 19, 32, 1024), F32)

    def params(limit):
        return pltpu.CompilerParams(vmem_limit_bytes=limit * mib)

    def cost(flops, data):
        return pl.CostEstimate(flops=flops, bytes_accessed=data, transcendentals=0)

    slots_shape = pltpu.SMEM((4,), jnp.int32)
    near_shape = pltpu.SMEM((4, 8), jnp.int32)
    raw, mate, migration, neighbours = pl.pallas_call(
        first_kernel,
        name="faces_and_leaver",
        out_shape=(pltpu.VMEM((4, 20, 32, 1024), F32), mate_shape, slots_shape, near_shape),
        in_specs=[SMEM, SMEM, HBM, HBM],
        out_specs=(VMEM, VMEM, SMEM, SMEM),
        scratch_shapes=[pltpu.VMEM((19, 10, 48, 128), F32), stage, dma((2, 2)), dma((4,)), dma((4,)), dma((8,))],
        compiler_params=params(8),
        cost_estimate=cost(20_000_000, 12_000_000),
    )(migration, neighbours, populations, solid_share)

    axes = ("gx", "gy")
    got = lax.ppermute(mate, axes, route(0, 1))

    out, streamed = pl.pallas_call(
        early_kernel,
        name="early_blocks",
        out_shape=(out_shape, stream_shape),
        in_specs=[SMEM, VMEM, VMEM],
        out_specs=(HBM, VMEM),
        scratch_shapes=[stage, dma((3, 8))],
        compiler_params=params(4),
        cost_estimate=cost(30_000_000, 16_000_000),
    )(migration, raw, mate)

    rise, fall = pl.pallas_call(
        select_kernel,
        name="select_faces",
        out_shape=(halo_shape, halo_shape),
        in_specs=[VMEM, VMEM, VMEM],
        out_specs=(VMEM, VMEM),
        scratch_shapes=[
            pltpu.VMEM((2, 2, 5, 32, 128), F32),
            pltpu.SMEM((8,), jnp.int32),
            pltpu.SMEM((8,), jnp.int32),
        ],
        compiler_params=params(4),
        cost_estimate=cost(1_000_000, 1_000_000),
    )(mate, got, streamed)
    high = lax.ppermute(fall, axes, route(-2, 0))
    low = lax.ppermute(rise, axes, route(2, 0))

    out, streamed, got = pl.pallas_call(
        late_kernel,
        name="late_blocks",
        out_shape=(out_shape, stream_shape, mate_shape),
        in_specs=[SMEM, SMEM] + [VMEM] * 5 + [HBM],
        out_specs=(HBM, VMEM, VMEM),
        input_output_aliases={7: 0, 3: 1, 5: 2},
        scratch_shapes=[
            stage,
            pltpu.VMEM((2, 10, 32, 128), F32),
            pltpu.VMEM((3, 2, 14, 8, 768), F32),
            pltpu.SMEM((8,), jnp.int32),
            dma((3, 8)), dma((8,)), dma((3, 2)), dma((4, 2)),
        ],
        compiler_params=params(6),
        cost_estimate=cost(30_000_000, 16_000_000),
    )(neighbours, migration, raw, streamed, mate, got, fall, out)

    out, _, _ = pl.pallas_call(
        last_kernel,
        name="outer_columns",
        out_shape=(out_shape, stream_shape, mate_shape),
        in_specs=[SMEM, SMEM] + [VMEM] * 5 + [HBM],
        out_specs=(HBM, VMEM, VMEM),
        input_output_aliases={7: 0, 6: 1, 5: 2},
        scratch_shapes=[
            pltpu.VMEM((3, 5, 32, 128), F32),
            pltpu.VMEM((3, 5, 32, 128), F32),
            pltpu.SMEM((24,), jnp.int32),
            dma((2,)), dma((3, 2)),
        ],
        compiler_params=params(6),
        cost_estimate=cost(1_000_000, 8_000_000),
    )(neighbours, migration, mate, low, high, got, streamed, out)
    return out


def solution(mesh):
    return jax.shard_map(
        on_device,
        mesh=mesh,
        in_specs=(
            P(("gx", "gy"), None, None, None),
            P(("gx", "gy"), None, None),
            P(("gx", "gy")),
            P(("gx", "gy"), None),
        ),
        out_specs=P(("gx", "gy"), None, None, None),
        check_vma=False,
    )
```
